128 devices in a mesh: chan: 64 (over z_hi, x, y, core), pix: 2 (over z_lo).
Axes of the slice: x: 4, y: 4, z: 4 (z_hi: 2, z_lo: 2; z = z_hi * 2 + z_lo), core: 2. Of those that a mesh axis runs over, the one named last changes fastest.
Arguments:
- pol_cube: bfloat16 [2, 2304, 8, 2048], P(None, 'chan', None, 'pix'), may hold values from -96 to 96
- phasor: bfloat16 [2, 2304, 512], P(None, 'chan'), may hold values from -1 to 1, as said below
- chan_weight: float32 [2304], P('chan'), may hold values from 0.3 to 9
- flags: int32 [2304, 8], P('chan'), may hold values 0 or 1
Outputs:
- depth_cube: bfloat16 [2, 1024, 8, 2, 512], P('pix', 'chan')
The draws below stay inside these ranges and needn't reach their ends.
Inputs may be any that keep to these rules, and one draw needn't show every extreme that they name: phasor[0] and phasor[1] are the cosine and sine of one angle.
All inputs are finite; a program needn't handle non-finite values. No bound on the sum of `flags` on one device may be relied on, other than what follows from the above.
Results may differ from the reference program's by a relative error of at most 0.0049.
Values may be sent and summed in bfloat16 or wider, within the bound.
A program may use at most 192 MiB of HBM per device.

```python
import jax
import jax.numpy as jnp

DEPTHS = 512
ROWS = 8
COLS_LOC = 1024
CHANNELS = 2304
COLS = 2048
N_PIX = 2


def draw_phasor(key, part):
    key = jax.random.fold_in(key, 11)
    angles = jax.random.uniform(key, (CHANNELS, DEPTHS), jnp.float32, -3.14159265, 3.14159265)
    return jnp.stack([jnp.cos(angles), jnp.sin(angles)], 0).astype(jnp.bfloat16)


def draw_chan_weight(key, part):
    key = jax.random.fold_in(key, 23)
    ramp = 1.0 + 2.0 * jnp.arange(CHANNELS, dtype=jnp.float32) / max(CHANNELS - 1, 1)
    factor = jax.random.uniform(key, (CHANNELS,), jnp.float32, 0.6, 1.6)
    return (ramp * factor).astype(jnp.float32)


def set_ends(entries, stream_key, least, largest):
    extent = entries.shape
    spot = [jax.random.randint(jax.random.fold_in(stream_key, axis), (), 0, extent[axis]) for axis in range(len(extent))]
    entries = entries.at[tuple(spot)].set(least)
    longest = extent.index(max(extent))
    spot[longest] = (spot[longest] + 1) % extent[longest]
    return entries.at[tuple(spot)].set(largest)


def levels(stream_key, dims, split, least, high):
    loudness, own = 1.0, jax.random.fold_in(stream_key, 6)
    for axis_at, parts in split:
        draws = jnp.exp(jax.random.uniform(jax.random.fold_in(own, axis_at), (parts,), jnp.float32, least / len(split), high / len(split)))
        loudness = loudness * jnp.repeat(draws, dims[axis_at] // parts).reshape([-1 if axis == axis_at else 1 for axis in range(len(dims))])
    return loudness


def centred(stream_key, extent, width, limit, cuts=(), held_as=jnp.bfloat16):
    values = width * jax.random.normal(stream_key, extent, jnp.float32)
    if cuts:
        values = values * levels(stream_key, extent, cuts, -0.22, 0.18)
    return jnp.clip(values, -limit, limit).astype(held_as)


def setup_inputs(seed: int = 0) -> dict:
    keys = jax.random.split(jax.random.key(seed), 5)
    return {
        "pol_cube": centred(keys[0], (2, CHANNELS, ROWS, COLS), 16.0, 96.0, ((1, 64), (3, 2))),
        "phasor": draw_phasor(jax.random.fold_in(keys[4], 71), 0),
        "chan_weight": draw_chan_weight(jax.random.fold_in(keys[4], 71), 0),
        "flags": set_ends((jax.random.randint(keys[3], (CHANNELS, ROWS), 0, 8) < 7).astype(jnp.int32), jax.random.fold_in(keys[3], 1), 0, 1),
    }


def reference(pol_cube, phasor, chan_weight, flags):
    weights = chan_weight[:, None] * flags.astype(jnp.float32)
    total = jnp.sum(weights, axis=0)
    weighted = (pol_cube.astype(jnp.float32) * weights[None, :, :, None]).astype(jnp.bfloat16)
    real_part = phasor[0]
    imag_part = phasor[1]
    matrix = jnp.stack([jnp.stack([real_part, imag_part], 1), jnp.stack([-imag_part, real_part], 1)], 0)
    terms = jnp.einsum("scrx,scod->xrod", weighted.astype(jnp.float32), matrix.astype(jnp.float32))
    result = terms / total[None, :, None, None]
    return result.reshape(N_PIX, COLS_LOC, ROWS, 2, DEPTHS).astype(jnp.bfloat16)
```

```python
import jax
import jax.numpy as jnp
from jax import lax
from jax.experimental import pallas as pl
from jax.experimental.pallas import tpu as pltpu
from jax.sharding import PartitionSpec as P

MESH = pl.DeviceIdType.MESH
F32 = jnp.float32
BF16 = jnp.bfloat16

X, Y = 4, 4
CH = 36
BODY = 32
TAIL = CH - BODY
ROWS1 = 2 * BODY + 16
ROWS2 = 2 * BODY


def tdot(a, b):
    return lax.dot_general(a, b, (((0,), (0,)), ((), ())), preferred_element_type=F32)


def kernel(
    pol, phasor, cw, flags_t, out,
    wb, stage, s1, s2, r1, r2, pa, pb, tw, part, d2d, zsend, zrecv, tots,
    bal_s, bal_r, pol_s, pol_r, ph_s, ph_r, tw_s, tw_r, d_s, d_r, z_s, z_r, t_s, t_r, loc,
):
    me = lax.axis_index("chan")
    pix = lax.axis_index("pix")
    core = lax.rem(me, 2)
    y = lax.rem(me // 2, Y)
    x = lax.rem(me // (2 * Y), X)
    zh = me // (2 * X * Y)

    def dev(zz, xx, yy, cc):
        return (((zz * X + xx) * Y + yy) * 2 + cc, pix)

    def plane(dx, dy):
        return dev(zh, lax.rem(x + dx, X), lax.rem(y + dy, Y), core)

    core_peer = dev(zh, x, y, 1 - core)
    z_peer = dev(1 - zh, x, y, core)
    offsets = [(dx, dy) for dx in range(X) for dy in range(Y) if dx or dy]

    barrier = pltpu.get_barrier_semaphore()
    for target in [plane(dx, dy) for dx, dy in offsets] + [core_peer, z_peer]:
        pl.semaphore_signal(barrier, inc=1, device_id=target, device_id_type=MESH)

    re = phasor[0].astype(F32)
    im = phasor[1].astype(F32)
    re_t, im_t = re[BODY:], im[BODY:]
    block = jnp.concatenate([re[:BODY], im[:BODY], re_t, -im_t, im_t, re_t], axis=0).astype(BF16)
    pa[0, 0] = block[:, :256]
    pb[0, 0] = block[:, 256:]

    w = cw[...] * flags_t[...].astype(F32)
    for c in range(CH):
        wb[c] = jnp.broadcast_to(w[:, c : c + 1], (8, 128))
    row_sum = jnp.sum(w, axis=1, keepdims=True)
    lane = lax.broadcasted_iota(jnp.int32, (8, 128), 1)
    sub = lax.broadcasted_iota(jnp.int32, (8, 128), 0)
    tw[0] = jnp.sum(jnp.where(lane // 16 == sub, row_sum, 0.0), axis=0, keepdims=True)

    pl.semaphore_wait(barrier, len(offsets) + 2)

    def rcopy(src, dst, ss, rs, target):
        return pltpu.make_async_remote_copy(
            src_ref=src, dst_ref=dst, send_sem=ss, recv_sem=rs,
            device_id=target, device_id_type=MESH,
        )

    ph = {}

    def phasor_send(half, buf, have, to):
        k = half * 16 + to[0] * 4 + to[1]
        hop = (to[0] - have[0], to[1] - have[1])
        c = rcopy(buf.at[have], buf.at[to], ph_s.at[k], ph_r.at[k], plane(*hop))
        c.start()
        ph[(half,) + to] = c

    near = [1, 3, 2]
    for d in near:
        phasor_send(0, pa, (0, 0), (d, 0))
        phasor_send(1, pb, (0, 0), (0, d))
    for d in near:
        phasor_send(0, pa, (0, 0), (0, d))
        phasor_send(1, pb, (0, 0), (d, 0))

    tw_copies = []
    for dx, dy in offsets:
        k = dx * 4 + dy
        c = rcopy(tw.at[0], tw.at[k], tw_s.at[k], tw_r.at[k], plane(dx, dy))
        c.start()
        tw_copies.append(c)

    lane_b = lax.broadcasted_iota(jnp.int32, (1, 128), 1)

    def relayout(first, dx):
        xx = lax.rem(x + dx, X)
        zz = 1 - zh if first else zh
        at = pl.multiple_of((zz * X + xx) * 128, 128)
        other = pl.multiple_of((zh * X + xx) * 128, 128)
        rows = ROWS1 if first else ROWS2
        dst = s1 if first else s2
        for s in range(2):
            v = pol[s, :BODY, :, pl.ds(at, 128)].astype(F32) * wb[:BODY]
            stage[pl.ds(s * 256, 256), :] = v.reshape(256, 128)
        if first:
            for h, at_h in enumerate((at, other)):
                for s in range(2):
                    v = pol[s, BODY:, :, pl.ds(at_h, 128)].astype(F32) * wb[BODY:]
                    stage[pl.ds(512 + h * 64 + s * 32, 32), :] = v.reshape(32, 128)
        for q in range(rows // 16):
            v = [stage[pl.ds(q * 128 + r, 16, stride=8), :] for r in range(8)]
            for k in range(3):
                m = 1 << k
                mask = jnp.broadcast_to((lane_b // (16 * m)) % 2 == 1, (16, 128))
                new = list(v)
                for a in range(8):
                    if a & m:
                        continue
                    b = a | m
                    new[a] = jnp.where(mask, pltpu.roll(v[b], 16 * m, 1), v[a])
                    new[b] = jnp.where(mask, v[b], pltpu.roll(v[a], 128 - 16 * m, 1))
                v = new
            for g in range(8):
                dst[dx, g // 2, pl.ds(q * 16, 16), pl.ds((g % 2) * 128, 128)] = v[g].astype(BF16)

    pol_copies = ([], [])

    def send_pol(first, dx):
        src, dst = (s1, r1) if first else (s2, r2)
        for dy in range(Y):
            if dx == 0 and dy == 0:
                c = pltpu.make_async_copy(src.at[0, y], dst.at[0], loc.at[0 if first else 1])
            else:
                k = (0 if first else 16) + dx * 4 + dy
                c = rcopy(
                    src.at[dx, lax.rem(y + dy, Y)], dst.at[dx * 4 + dy],
                    pol_s.at[k], pol_r.at[k], plane(dx, dy),
                )
            c.start()
            pol_copies[0 if first else 1].append(c)

    for dx in (1, 3, 0, 2):
        relayout(True, dx)
        send_pol(True, dx)

    for d in near:
        ph[(0, d, 0)].wait_recv()
        for e in near:
            phasor_send(0, pa, (d, 0), (d, e))
        ph[(1, 0, d)].wait_recv()
        for e in near:
            phasor_send(1, pb, (0, d), (e, d))

    for dx in (1, 3, 0, 2):
        relayout(False, dx)
        send_pol(False, dx)

    for c in tw_copies:
        c.wait_recv()
    total = jnp.sum(tw[...], axis=0)
    tots[0] = total
    ct = rcopy(tots.at[0], tots.at[1], t_s.at[0], t_r.at[0], core_peer)
    ct.start()

    for d in range(X):
        for e in range(Y):
            if d or e:
                for half in range(2):
                    if not (half == 0 and e == 0) and not (half == 1 and d == 0):
                        ph[(half, d, e)].wait_recv()
    for c in pol_copies[0]:
        if c is pol_copies[0][8]:
            c.wait()
        else:
            c.wait_recv()

    row16 = lax.broadcasted_iota(jnp.int32, (256, 256), 0) % 16

    def contract(first, n):
        src = r1 if first else r2
        k, half = n // 2, n % 2
        p = (pa, pb)[half]
        w0 = src[:, :BODY].reshape(16 * BODY, 256)
        w1 = src[:, BODY : 2 * BODY].reshape(16 * BODY, 256)
        pr = p[:, :, :BODY].reshape(16 * BODY, 256)
        pi = p[:, :, BODY : 2 * BODY].reshape(16 * BODY, 256)
        lt = r1[:, 2 * BODY :].reshape(256, 256).astype(F32)
        pt = p[:, :, 2 * BODY :].reshape(256, 256)
        lt = jnp.where((row16 < 8) == first, lt, 0.0).astype(BF16)
        if first == (k == 1):
            shifted = pt.astype(F32)
            cut = 8 if first else 248
            pt = jnp.concatenate([shifted[cut:], shifted[:cut]], axis=0).astype(BF16)
        if k == 0:
            o = tdot(w0, pr) - tdot(w1, pi)
        else:
            o = tdot(w0, pi) + tdot(w1, pr)
        return o + tdot(lt, pt)

    mine = pl.multiple_of(core * 128, 128)
    theirs = pl.multiple_of((1 - core) * 128, 128)

    def spread(first, n):
        k = (0 if first else 4) + n
        part[k] = contract(first, n)
        c = rcopy(part.at[k, pl.ds(theirs, 128)], d2d.at[k], d_s.at[k], d_r.at[k], core_peer)
        c.start()
        return c

    d_copies = [spread(True, n) for n in range(4)]

    ct.wait_recv()
    plane_total = tots[0] + tots[1]
    tots[2] = plane_total
    cz = rcopy(tots.at[2], tots.at[3], t_s.at[1], t_r.at[1], z_peer)
    cz.start()

    z_copies = []
    for n in range(4):
        d_copies[n].wait_recv()
        zsend[n] = (part[n, pl.ds(mine, 128)] + d2d[n]).astype(BF16)
        c = rcopy(zsend.at[n], zrecv.at[n], z_s.at[n], z_r.at[n], z_peer)
        c.start()
        z_copies.append(c)

    for c in pol_copies[1]:
        if c is pol_copies[1][8]:
            c.wait()
        else:
            c.wait_recv()
    d_copies += [spread(False, n) for n in range(4)]

    cz.wait_recv()
    total = tots[2] + tots[3]
    ri = lax.broadcasted_iota(jnp.int32, (128, 128), 0)
    ci = lax.broadcasted_iota(jnp.int32, (128, 128), 1)
    column = jnp.sum(jnp.where(ri == ci, total, 0.0), axis=1, keepdims=True)
    for n in range(4):
        d_copies[4 + n].wait_recv()
        z_copies[n].wait_recv()
        summed = part[4 + n, pl.ds(mine, 128)] + d2d[4 + n] + zrecv[n].astype(F32)
        out[:, pl.ds(n * 256, 256)] = (summed / column).astype(BF16)

    for c in list(ph.values()) + tw_copies + [ct, cz] + d_copies + z_copies:
        c.wait_send()
    for group in pol_copies:
        for i, c in enumerate(group):
            if i != 8:
                c.wait_send()


def body(pol_cube, phasor, chan_weight, flags):
    vmem = pl.BlockSpec(memory_space=pltpu.VMEM)
    dma = pltpu.SemaphoreType.DMA
    out = pl.pallas_call(
        kernel,
        out_shape=jax.ShapeDtypeStruct((128, 1024), BF16),
        in_specs=[vmem] * 4,
        out_specs=vmem,
        scratch_shapes=[
            pltpu.VMEM((CH, 8, 128), F32),
            pltpu.VMEM((ROWS1 * 8, 128), F32),
            pltpu.VMEM((X, Y, ROWS1, 256), BF16),
            pltpu.VMEM((X, Y, ROWS2, 256), BF16),
            pltpu.VMEM((16, ROWS1, 256), BF16),
            pltpu.VMEM((16, ROWS2, 256), BF16),
            pltpu.VMEM((X, Y, ROWS1, 256), BF16),
            pltpu.VMEM((X, Y, ROWS1, 256), BF16),
            pltpu.VMEM((16, 1, 128), F32),
            pltpu.VMEM((8, 256, 256), F32),
            pltpu.VMEM((8, 128, 256), F32),
            pltpu.VMEM((4, 128, 256), BF16),
            pltpu.VMEM((4, 128, 256), BF16),
            pltpu.VMEM((4, 1, 128), F32),
            dma((1,)), dma((1,)),
            dma((32,)), dma((32,)),
            dma((32,)), dma((32,)),
            dma((16,)), dma((16,)),
            dma((8,)), dma((8,)),
            dma((4,)), dma((4,)),
            dma((2,)), dma((2,)),
            dma((2,)),
        ],
        compiler_params=pltpu.CompilerParams(
            collective_id=0, has_side_effects=True, vmem_limit_bytes=40 * 2**20
        ),
        cost_estimate=pl.CostEstimate(
            flops=2 * 512 * 1152 * 1024, bytes_accessed=2**21, transcendentals=0
        ),
        name="exchange",
    )(pol_cube, phasor, chan_weight[None, :], flags.T)
    return out.reshape(8, 16, 2, 512).transpose(1, 0, 2, 3)[None]


def solution(mesh):
    placed = (P(None, "chan", None, "pix"), P(None, "chan", None), P("chan"), P("chan", None))
    return jax.shard_map(
        body,
        mesh=mesh,
        in_specs=placed,
        out_specs=P("pix", "chan", None, None, None),
        check_vma=False,
    )
```

```python
import jax
import jax.numpy as jnp
from jax import lax
from jax.experimental import pallas as pl
from jax.experimental.pallas import tpu as pltpu
from jax.sharding import PartitionSpec as P

MESH = pl.DeviceIdType.MESH
F32 = jnp.float32
BF16 = jnp.bfloat16

X, Y = 4, 4
CH = 36
BODY = 32
ROWS1 = 2 * BODY + 16
ROWS2 = 2 * BODY
PH_ROWS = ROWS1 + ROWS2


def tdot(a, b):
    return lax.dot_general(a, b, (((0,), (0,)), ((), ())), preferred_element_type=F32)


def kernel(
    pol_hbm, phasor_hbm, cw_hbm, flags_hbm, out,
    pol, phasor, cw, flags_t, wb, s1, s2, r1, r2, ph, tw, part, d2d, zsend, zrecv, tots,
    in_sem, pol_s, pol_r, ph_s, ph_r, tw_s, tw_r, d_s, d_r, z_s, z_r, t_s, t_r,
):
    me = lax.axis_index("chan")
    pix = lax.axis_index("pix")
    core = lax.rem(me, 2)
    y = lax.rem(me // 2, Y)
    x = lax.rem(me // (2 * Y), X)
    zh = me // (2 * X * Y)

    def dev(zz, xx, yy, cc):
        return (((zz * X + xx) * Y + yy) * 2 + cc, pix)

    def plane(dx, dy):
        return dev(zh, lax.rem(x + dx, X), lax.rem(y + dy, Y), core)

    core_peer = dev(zh, x, y, 1 - core)
    z_peer = dev(1 - zh, x, y, core)
    offsets = [(dx, dy) for dx in range(X) for dy in range(Y) if dx or dy]

    barrier = pltpu.get_barrier_semaphore()
    peers = [plane(dx, dy) for dx, dy in offsets] + [core_peer, z_peer]
    for target in peers:
        pl.semaphore_signal(barrier, inc=1, device_id=target, device_id_type=MESH)

    loads = [
        pltpu.make_async_copy(a, b, in_sem.at[i])
        for i, (a, b) in enumerate(
            ((flags_hbm, flags_t), (cw_hbm, cw), (phasor_hbm, phasor), (pol_hbm, pol))
        )
    ]
    for c in loads:
        c.start()

    i = lax.broadcasted_iota(jnp.int32, (256, 256), 0)
    j = lax.broadcasted_iota(jnp.int32, (256, 256), 1)
    order = jnp.where((i % 32) * 8 + i // 32 == j, 1.0, 0.0).astype(BF16)
    i, j = i[:128, :128], j[:128, :128]
    order_t = jnp.where((i % 16) * 8 + i // 16 == j, 1.0, 0.0).astype(BF16)

    loads[0].wait()
    loads[1].wait()
    w = cw[...] * flags_t[...].astype(F32)
    for c in range(CH):
        wb[c] = jnp.broadcast_to(w[:, c : c + 1], (8, 128))
    row_sum = jnp.sum(w, axis=1, keepdims=True)
    lane = lax.broadcasted_iota(jnp.int32, (8, 128), 1)
    sub = lax.broadcasted_iota(jnp.int32, (8, 128), 0)
    tw[0] = jnp.sum(jnp.where(lane // 16 == sub, row_sum, 0.0), axis=0, keepdims=True)

    loads[2].wait()
    both = phasor[...].astype(F32)
    re, im = both[:, 0], both[:, 1]
    tails = [jnp.concatenate([re[BODY:, h : h + 256], -im[BODY:, h : h + 256]], axis=0) for h in (0, 256)]
    block = jnp.concatenate(
        [re[:BODY, :256], im[:BODY, :256]] + tails + [re[:BODY, 256:], im[:BODY, 256:]], axis=0
    ).astype(BF16)
    ph[0, 0, 0] = block[:, :128]
    ph[1, 0, 0] = block[:, 128:]

    lane_b = lax.broadcasted_iota(jnp.int32, (1, 128), 1)

    def swap_blocks(v):
        for k in range(3):
            m = 1 << k
            mask = jnp.broadcast_to((lane_b // (16 * m)) % 2 == 1, v[0].shape)
            new = list(v)
            for a in range(8):
                if a & m:
                    continue
                b = a | m
                new[a] = jnp.where(mask, pltpu.roll(v[b], 16 * m, 1), v[a])
                new[b] = jnp.where(mask, v[b], pltpu.roll(v[a], 128 - 16 * m, 1))
            v = new
        return v

    def weighted(s, chans, at):
        v = pol[s, chans, :, pl.ds(at, 128)].astype(F32) * wb[chans]
        return v.reshape(-1, 128).astype(BF16)

    def regroup(matrix, v, rows):
        u = jnp.dot(matrix, v, preferred_element_type=F32).astype(BF16)
        return swap_blocks([u[r * rows : (r + 1) * rows] for r in range(8)])

    def relayout(first, dx):
        xx = lax.rem(x + dx, X)
        far = pl.multiple_of(((1 - zh) * X + xx) * 128, 128)
        near = pl.multiple_of((zh * X + xx) * 128, 128)
        dst = s1 if first else s2
        for s in range(2):
            v = regroup(order, weighted(s, slice(0, BODY), far if first else near), BODY)
            for g in range(8):
                dst[dx, g // 2, pl.ds(s * BODY, BODY), pl.ds((g % 2) * 128, 128)] = v[g]
        if first:
            v = [weighted(s, slice(BODY, CH), at) for at in (far, near) for s in range(2)]
            v = regroup(order_t, jnp.concatenate(v, axis=0), 16)
            for g in range(8):
                dst[dx, g // 2, pl.ds(2 * BODY, 16), pl.ds((g % 2) * 128, 128)] = v[g]

    loads[3].wait()
    near_x = (1, 3, 0, 2)
    for dx in near_x:
        relayout(True, dx)

    pl.semaphore_wait(barrier, len(peers))

    def rcopy(src, dst, ss, rs, target):
        return pltpu.make_async_remote_copy(
            src_ref=src, dst_ref=dst, send_sem=ss, recv_sem=rs,
            device_id=target, device_id_type=MESH,
        )

    def wait_for(view, sem):
        pltpu.make_async_copy(view, view, sem).wait()

    ring = (1, 3, 2)
    rest = pl.ds(1, 3)
    rows_a, rows_b = pl.ds(0, ROWS1), pl.ds(ROWS1, ROWS2)
    arrive = [
        ph.at[0, rest, 0],
        ph.at[1, 0, rest],
        ph.at[0, 0, rest],
        ph.at[1, rest, 0],
        ph.at[0, rest, rest, rows_a],
        ph.at[1, rest, rest, rows_a],
        ph.at[0, rest, rest, rows_b],
        ph.at[1, rest, rest, rows_b],
    ]
    for d in ring:
        rcopy(ph.at[0, 0, 0], ph.at[0, d, 0], ph_s.at[0], ph_r.at[0], plane(d, 0)).start()
        rcopy(ph.at[1, 0, 0], ph.at[1, 0, d], ph_s.at[1], ph_r.at[1], plane(0, d)).start()
    for d in ring:
        rcopy(ph.at[0, 0, 0], ph.at[0, 0, d], ph_s.at[2], ph_r.at[2], plane(0, d)).start()
        rcopy(ph.at[1, 0, 0], ph.at[1, d, 0], ph_s.at[3], ph_r.at[3], plane(d, 0)).start()

    def send_pol(first, dx):
        q = 0 if first else 1
        src, dst = (s1, r1) if first else (s2, r2)
        for dy in range(Y):
            if dx == 0 and dy == 0:
                pltpu.make_async_copy(src.at[0, y], dst.at[0], in_sem.at[4 + q]).start()
            else:
                rcopy(
                    src.at[dx, lax.rem(y + dy, Y)], dst.at[dx * 4 + dy],
                    pol_s.at[q], pol_r.at[q], plane(dx, dy),
                ).start()

    for dx, dy in offsets:
        k = dx * 4 + dy
        rcopy(tw.at[0], tw.at[k], tw_s.at[0], tw_r.at[0], plane(dx, dy)).start()

    for dx in near_x:
        send_pol(True, dx)

    def forward(q, strip, rows):
        for d in ring:
            if strip == 0:
                c = rcopy(
                    ph.at[0, rest, 0, rows], ph.at[0, rest, d, rows],
                    ph_s.at[q], ph_r.at[q], plane(0, d),
                )
            else:
                c = rcopy(
                    ph.at[1, 0, rest, rows], ph.at[1, d, rest, rows],
                    ph_s.at[q], ph_r.at[q], plane(d, 0),
                )
            c.start()

    wait_for(arrive[0], ph_r.at[0])
    forward(4, 0, rows_a)
    wait_for(arrive[1], ph_r.at[1])
    forward(5, 1, rows_a)
    forward(6, 0, rows_b)
    forward(7, 1, rows_b)

    for dx in near_x:
        relayout(False, dx)
        send_pol(False, dx)

    def contract(first, half):
        src = r1 if first else r2
        at = 0 if half == 0 else ROWS1
        w0 = src[:, :BODY].reshape(16 * BODY, 256)
        w1 = src[:, BODY : 2 * BODY].reshape(16 * BODY, 256)
        lt = r1[:, 2 * BODY :].astype(F32)
        lt = lt[:, :8] if first else lt[:, 8:]
        lt = lt.reshape(128, 256).astype(BF16)

        def lanes(lo, hi):
            return jnp.concatenate(
                [ph[s, :, :, lo:hi].reshape(-1, 128) for s in range(2)], axis=1
            )

        pr = lanes(at, at + BODY)
        pi = lanes(at + BODY, at + 2 * BODY)
        pt = lanes(2 * BODY, ROWS1).reshape(16, 16, 256).astype(F32)
        pt = pt[:, :8] if half == 0 else pt[:, 8:]
        turned = jnp.concatenate([-pt[:, 4:], pt[:, :4]], axis=1)
        pt = pt.reshape(128, 256).astype(BF16)
        turned = turned.reshape(128, 256).astype(BF16)
        yield tdot(w0, pr) - tdot(w1, pi) + tdot(lt, pt)
        yield tdot(w0, pi) + tdot(w1, pr) + tdot(lt, turned)

    mine = pl.multiple_of(core * 128, 128)
    theirs = pl.multiple_of((1 - core) * 128, 128)

    def spread(first, half):
        copies = []
        for k, value in enumerate(contract(first, half)):
            n = (0 if first else 4) + half * 2 + k
            part[n] = value
            c = rcopy(part.at[n, pl.ds(theirs, 128)], d2d.at[n], d_s.at[n], d_r.at[n], core_peer)
            c.start()
            copies.append(c)
        return copies

    d_copies, z_copies = [], []
    for g in (2, 3, 4, 5):
        wait_for(arrive[g], ph_r.at[g])
    wait_for(r1.at[pl.ds(1, 15)], pol_r.at[0])
    wait_for(r1.at[0], in_sem.at[4])
    for half in range(2):
        if half == 1:
            for g in (6, 7):
                wait_for(arrive[g], ph_r.at[g])
        d_copies += spread(True, half)
        for n in (half * 2, half * 2 + 1):
            d_copies[n].wait_recv()
            zsend[n] = (part[n, pl.ds(mine, 128)] + d2d[n]).astype(BF16)
            c = rcopy(zsend.at[n], zrecv.at[n], z_s.at[n], z_r.at[n], z_peer)
            c.start()
            z_copies.append(c)

    wait_for(tw.at[pl.ds(1, 15)], tw_r.at[0])
    tots[0] = jnp.sum(tw[...], axis=0)
    ct = rcopy(tots.at[0], tots.at[1], t_s.at[0], t_r.at[0], core_peer)
    ct.start()
    ct.wait_recv()
    tots[2] = tots[0] + tots[1]
    cz = rcopy(tots.at[2], tots.at[3], t_s.at[1], t_r.at[1], z_peer)
    cz.start()

    wait_for(r2.at[pl.ds(1, 15)], pol_r.at[1])
    wait_for(r2.at[0], in_sem.at[5])
    d_copies += spread(False, 0) + spread(False, 1)
    cz.wait_recv()
    total = tots[2] + tots[3]
    ri = lax.broadcasted_iota(jnp.int32, (128, 128), 0)
    ci = lax.broadcasted_iota(jnp.int32, (128, 128), 1)
    column = jnp.sum(jnp.where(ri == ci, total, 0.0), axis=1, keepdims=True)
    for n in range(4):
        z_copies[n].wait_recv()
        d_copies[4 + n].wait_recv()
        summed = part[4 + n, pl.ds(mine, 128)] + d2d[4 + n] + zrecv[n].astype(F32)
        out[:, pl.ds((n % 2) * 512 + (n // 2) * 256, 256)] = (summed / column).astype(BF16)

    for c in [ct, cz] + d_copies + z_copies:
        c.wait_send()
    for g in range(8):
        wait_for(arrive[g], ph_s.at[g])
    wait_for(r1.at[pl.ds(1, 15)], pol_s.at[0])
    wait_for(r2.at[pl.ds(1, 15)], pol_s.at[1])
    wait_for(tw.at[pl.ds(1, 15)], tw_s.at[0])


def body(pol_cube, phasor, chan_weight, flags):
    vmem = pltpu.VMEM
    dma = pltpu.SemaphoreType.DMA
    out = pl.pallas_call(
        kernel,
        out_shape=jax.ShapeDtypeStruct((128, 1024), BF16),
        in_specs=[pl.BlockSpec(memory_space=pltpu.HBM)] * 4,
        out_specs=pl.BlockSpec(memory_space=vmem),
        scratch_shapes=[
            vmem((2, CH, 8, 1024), BF16),
            vmem((CH, 2, 512), BF16),
            vmem((1, CH), F32),
            vmem((8, CH), jnp.int32),
            vmem((CH, 8, 128), F32),
            vmem((X, Y, ROWS1, 256), BF16),
            vmem((X, Y, ROWS2, 256), BF16),
            vmem((16, ROWS1, 256), BF16),
            vmem((16, ROWS2, 256), BF16),
            vmem((2, X, Y, PH_ROWS, 128), BF16),
            vmem((16, 1, 128), F32),
            vmem((8, 256, 256), F32),
            vmem((8, 128, 256), F32),
            vmem((4, 128, 256), BF16),
            vmem((4, 128, 256), BF16),
            vmem((4, 1, 128), F32),
            dma((6,)),
            dma((2,)), dma((2,)),
            dma((8,)), dma((8,)),
            dma((1,)), dma((1,)),
            dma((8,)), dma((8,)),
            dma((4,)), dma((4,)),
            dma((2,)), dma((2,)),
        ],
        compiler_params=pltpu.CompilerParams(
            collective_id=0, has_side_effects=True, vmem_limit_bytes=62 * 2**20
        ),
        cost_estimate=pl.CostEstimate(
            flops=2 * 512 * 1152 * 1024, bytes_accessed=2**21, transcendentals=0
        ),
        name="exchange",
    )(pol_cube, phasor.transpose(1, 0, 2), chan_weight[None, :], flags.T)
    return out.reshape(8, 16, 2, 512).transpose(1, 0, 2, 3)[None]


def solution(mesh):
    placed = (P(None, "chan", None, "pix"), P(None, "chan", None), P("chan"), P("chan", None))
    return jax.shard_map(
        body,
        mesh=mesh,
        in_specs=placed,
        out_specs=P("pix", "chan", None, None, None),
        check_vma=False,
    )
```

```python
import jax
import jax.numpy as jnp
from jax import lax
from jax.experimental import pallas as pl
from jax.experimental.pallas import tpu as pltpu
from jax.sharding import PartitionSpec as P

MESH = pl.DeviceIdType.MESH
F32 = jnp.float32
BF16 = jnp.bfloat16

X, Y = 4, 4
SPREAD = [(dx, dy) for dx in (1, 3, 0, 2) for dy in range(Y) if dx or dy]
CH = 36
BODY = 32
ROWS1 = 2 * BODY + 16
ROWS2 = 2 * BODY
PH_ROWS = ROWS1 + ROWS2


def tdot(a, b):
    return lax.dot_general(a, b, (((0,), (0,)), ((), ())), preferred_element_type=F32)


def kernel(
    pol_hbm, phasor_hbm, cw_hbm, flags_hbm, out,
    pol, phasor, cw, flags_t, order_o, wb, s1, s2, r1, r2, ph, tw, part, d2d, zsend, zrecv, tots,
    in_sem, pol_s, pol_r, ph_s, ph_r, tw_s, tw_r, d_s, d_r, z_s, z_r, t_s, t_r, ready,
):
    me = lax.axis_index("chan")
    pix = lax.axis_index("pix")
    core = lax.rem(me, 2)
    y = lax.rem(me // 2, Y)
    x = lax.rem(me // (2 * Y), X)
    zh = me // (2 * X * Y)

    def dev(zz, xx, yy, cc):
        return (((zz * X + xx) * Y + yy) * 2 + cc, pix)

    def plane(dx, dy):
        return dev(zh, lax.rem(x + dx, X), lax.rem(y + dy, Y), core)

    core_peer = dev(zh, x, y, 1 - core)
    z_peer = dev(1 - zh, x, y, core)
    offsets = [(dx, dy) for dx in range(X) for dy in range(Y) if dx or dy]

    barrier = pltpu.get_barrier_semaphore()
    peers = [plane(dx, dy) for dx, dy in offsets] + [core_peer]
    for target in peers:
        pl.semaphore_signal(barrier, inc=1, device_id=target, device_id_type=MESH)

    @pl.when(zh == 0)
    def _():
        pl.semaphore_signal(barrier, inc=1, device_id=z_peer, device_id_type=MESH)

    loads = [
        pltpu.make_async_copy(a, b, in_sem.at[i])
        for i, (a, b) in enumerate(
            ((flags_hbm, flags_t), (cw_hbm, cw), (phasor_hbm, phasor), (pol_hbm, pol))
        )
    ]
    for c in loads:
        c.start()

    i = lax.broadcasted_iota(jnp.int32, (256, 256), 0)
    j = lax.broadcasted_iota(jnp.int32, (256, 256), 1)
    order = jnp.where((i % 32) * 8 + i // 32 == j, 1.0, 0.0).astype(BF16)
    i, j = i[:128, :128], j[:128, :128]
    order_t = jnp.where((i % 16) * 8 + i // 16 == j, 1.0, 0.0).astype(BF16)

    i = lax.broadcasted_iota(jnp.int32, (256, 128), 0)
    j = lax.broadcasted_iota(jnp.int32, (256, 128), 1)
    at_row = (i // 2) % 8 * 16 + i // 16 == j
    for k in range(2):
        order_o[k] = jnp.where(at_row & (i % 2 == k), 1.0, 0.0).astype(BF16)

    loads[0].wait()
    loads[1].wait()
    w = cw[...] * flags_t[...].astype(F32)
    for c in range(CH):
        wb[c] = jnp.broadcast_to(w[:, c : c + 1], (8, 128))
    row_sum = jnp.sum(w, axis=1, keepdims=True)
    lane = lax.broadcasted_iota(jnp.int32, (8, 128), 1)
    sub = lax.broadcasted_iota(jnp.int32, (8, 128), 0)
    tw[0] = jnp.sum(jnp.where(lane // 16 == sub, row_sum, 0.0), axis=0, keepdims=True)

    loads[2].wait()
    both = phasor[...].astype(F32)
    re, im = both[:, 0], both[:, 1]
    tails = [jnp.concatenate([re[BODY:, h : h + 256], -im[BODY:, h : h + 256]], axis=0) for h in (0, 256)]
    block = jnp.concatenate(
        [re[:BODY, :256], im[:BODY, :256]] + tails + [re[:BODY, 256:], im[:BODY, 256:]], axis=0
    ).astype(BF16)
    ph[0, 0, 0] = block[:, :128]
    ph[1, 0, 0] = block[:, 128:]

    lane_b = lax.broadcasted_iota(jnp.int32, (1, 128), 1)

    def swap_blocks(v):
        for k in range(3):
            m = 1 << k
            mask = jnp.broadcast_to((lane_b // (16 * m)) % 2 == 1, v[0].shape)
            new = list(v)
            for a in range(8):
                if a & m:
                    continue
                b = a | m
                new[a] = jnp.where(mask, pltpu.roll(v[b], 16 * m, 1), v[a])
                new[b] = jnp.where(mask, v[b], pltpu.roll(v[a], 128 - 16 * m, 1))
            v = new
        return v

    def weighted(s, chans, at):
        v = pol[s, chans, :, pl.ds(at, 128)].astype(F32) * wb[chans]
        return v.reshape(-1, 128).astype(BF16)

    def regroup(matrix, v, rows):
        u = jnp.dot(matrix, v, preferred_element_type=F32).astype(BF16)
        return swap_blocks([u[r * rows : (r + 1) * rows] for r in range(8)])

    def relayout(first, dx):
        xx = lax.rem(x + dx, X)
        far = pl.multiple_of(((1 - zh) * X + xx) * 128, 128)
        near = pl.multiple_of((zh * X + xx) * 128, 128)
        dst = s1 if first else s2
        for s in range(2):
            v = regroup(order, weighted(s, slice(0, BODY), far if first else near), BODY)
            for g in range(8):
                dst[dx, g // 2, pl.ds(s * BODY, BODY), pl.ds((g % 2) * 128, 128)] = v[g]
        if first:
            v = [weighted(s, slice(BODY, CH), at) for at in (far, near) for s in range(2)]
            v = regroup(order_t, jnp.concatenate(v, axis=0), 16)
            for g in range(8):
                dst[dx, g // 2, pl.ds(2 * BODY, 16), pl.ds((g % 2) * 128, 128)] = v[g]

    loads[3].wait()
    near_x = (1, 3, 0, 2)
    for dx in near_x:
        relayout(True, dx)

    pl.semaphore_wait(barrier, len(peers) + zh)

    @pl.when(zh == 1)
    def _():
        pl.semaphore_signal(ready, inc=1, device_id=z_peer, device_id_type=MESH)

    def rcopy(src, dst, ss, rs, target):
        return pltpu.make_async_remote_copy(
            src_ref=src, dst_ref=dst, send_sem=ss, recv_sem=rs,
            device_id=target, device_id_type=MESH,
        )

    def wait_for(view, sem):
        pltpu.make_async_copy(view, view, sem).wait()

    ring = (1, 3, 2)
    rest = pl.ds(1, 3)
    rows_a, rows_b = pl.ds(0, ROWS1), pl.ds(ROWS1, ROWS2)
    arrive = [
        ph.at[0, rest, 0],
        ph.at[1, 0, rest],
        ph.at[0, 0, rest],
        ph.at[1, rest, 0],
        ph.at[0, rest, rest, rows_a],
        ph.at[1, rest, rest, rows_a],
        ph.at[0, rest, rest, rows_b],
        ph.at[1, rest, rest, rows_b],
    ]
    for d in ring:
        rcopy(ph.at[0, 0, 0], ph.at[0, d, 0], ph_s.at[0], ph_r.at[0], plane(d, 0)).start()
        rcopy(ph.at[1, 0, 0], ph.at[1, 0, d], ph_s.at[1], ph_r.at[1], plane(0, d)).start()
    for d in ring:
        rcopy(ph.at[0, 0, 0], ph.at[0, 0, d], ph_s.at[2], ph_r.at[2], plane(0, d)).start()
        rcopy(ph.at[1, 0, 0], ph.at[1, d, 0], ph_s.at[3], ph_r.at[3], plane(d, 0)).start()

    def send_pol(first, dx, dy):
        q = 0 if first else 1
        src, dst = (s1, r1) if first else (s2, r2)
        rcopy(
            src.at[dx, lax.rem(y + dy, Y)], dst.at[dx * 4 + dy],
            pol_s.at[q], pol_r.at[q], plane(dx, dy),
        ).start()

    pltpu.make_async_copy(s1.at[0, y], r1.at[0], in_sem.at[4]).start()
    for dx, dy in offsets:
        k = dx * 4 + dy
        rcopy(tw.at[0], tw.at[k], tw_s.at[0], tw_r.at[0], plane(dx, dy)).start()

    for dx, dy in SPREAD:
        send_pol(True, dx, dy)

    def forward(q, strip, rows):
        for d in ring:
            if strip == 0:
                c = rcopy(
                    ph.at[0, rest, 0, rows], ph.at[0, rest, d, rows],
                    ph_s.at[q], ph_r.at[q], plane(0, d),
                )
            else:
                c = rcopy(
                    ph.at[1, 0, rest, rows], ph.at[1, d, rest, rows],
                    ph_s.at[q], ph_r.at[q], plane(d, 0),
                )
            c.start()

    wait_for(arrive[0], ph_r.at[0])
    forward(4, 0, rows_a)
    wait_for(arrive[1], ph_r.at[1])
    forward(5, 1, rows_a)
    forward(6, 0, rows_b)
    forward(7, 1, rows_b)

    for dx in near_x:
        relayout(False, dx)
    pltpu.make_async_copy(s2.at[0, y], r2.at[0], in_sem.at[5]).start()
    for dx, dy in SPREAD:
        send_pol(False, dx, dy)

    wait_for(tw.at[pl.ds(1, 15)], tw_r.at[0])
    tots[0] = jnp.sum(tw[...], axis=0)
    ct = rcopy(tots.at[0], tots.at[1], t_s.at[0], t_r.at[0], core_peer)
    ct.start()

    def contract(first, half):
        src = r1 if first else r2
        at = 0 if half == 0 else ROWS1
        w0 = src[:, :BODY].reshape(16 * BODY, 256)
        w1 = src[:, BODY : 2 * BODY].reshape(16 * BODY, 256)
        lt = r1[:, 2 * BODY :].astype(F32)
        lt = lt[:, :8] if first else lt[:, 8:]
        lt = lt.reshape(128, 256).astype(BF16)

        def lanes(lo, hi):
            return jnp.concatenate(
                [ph[s, :, :, lo:hi].reshape(-1, 128) for s in range(2)], axis=1
            )

        pr = lanes(at, at + BODY)
        pi = lanes(at + BODY, at + 2 * BODY)
        pt = lanes(2 * BODY, ROWS1).reshape(16, 16, 256).astype(F32)
        pt = pt[:, :8] if half == 0 else pt[:, 8:]
        turned = jnp.concatenate([-pt[:, 4:], pt[:, :4]], axis=1)
        pt = pt.reshape(128, 256).astype(BF16)
        turned = turned.reshape(128, 256).astype(BF16)
        yield tdot(w0, pr) - tdot(w1, pi) + tdot(lt, pt)
        yield tdot(w0, pi) + tdot(w1, pr) + tdot(lt, turned)

    mine = pl.multiple_of(core * 128, 128)
    theirs = pl.multiple_of((1 - core) * 128, 128)

    def spread(first, half):
        copies = []
        for k, value in enumerate(contract(first, half)):
            n = (0 if first else 4) + half * 2 + k
            part[n] = value
            c = rcopy(part.at[n, pl.ds(theirs, 128)], d2d.at[n], d_s.at[n], d_r.at[n], core_peer)
            c.start()
            copies.append(c)
        return copies

    d_copies, z_copies = [], []
    for g in (2, 3, 4, 5):
        wait_for(arrive[g], ph_r.at[g])
    wait_for(r1.at[pl.ds(1, 15)], pol_r.at[0])
    wait_for(r1.at[0], in_sem.at[4])
    @pl.when(zh == 0)
    def _():
        pl.semaphore_wait(ready, 1)

    for half in range(2):
        if half == 1:
            for g in (6, 7):
                wait_for(arrive[g], ph_r.at[g])
        d_copies += spread(True, half)
        if half == 0:
            ct.wait_recv()
            tots[2] = tots[0] + tots[1]
            cz = rcopy(tots.at[2], tots.at[3], t_s.at[1], t_r.at[1], z_peer)
            cz.start()
        for n in (half * 2, half * 2 + 1):
            d_copies[n].wait_recv()
            zsend[n] = (part[n, pl.ds(mine, 128)] + d2d[n]).astype(BF16)
            c = rcopy(zsend.at[n], zrecv.at[n], z_s.at[n], z_r.at[n], z_peer)
            c.start()
            z_copies.append(c)

    wait_for(r2.at[pl.ds(1, 15)], pol_r.at[1])
    wait_for(r2.at[0], in_sem.at[5])
    d_copies += spread(False, 0) + spread(False, 1)
    cz.wait_recv()
    total = tots[2] + tots[3]
    ri = lax.broadcasted_iota(jnp.int32, (128, 128), 0)
    ci = lax.broadcasted_iota(jnp.int32, (128, 128), 1)
    column = jnp.sum(jnp.where(ri == ci, total, 0.0), axis=1, keepdims=True)
    for half in range(2):
        rows = 0.0
        for k in range(2):
            n = half * 2 + k
            z_copies[n].wait_recv()
            d_copies[4 + n].wait_recv()
            summed = part[4 + n, pl.ds(mine, 128)] + d2d[4 + n] + zrecv[n].astype(F32)
            value = (summed / column).astype(BF16)
            rows = rows + jnp.dot(order_o[k], value, preferred_element_type=F32)
        out[:, :, pl.ds(half * 256, 256)] = rows.astype(BF16).reshape(128, 2, 256)

    for c in [ct, cz] + d_copies + z_copies:
        c.wait_send()
    for g in range(8):
        wait_for(arrive[g], ph_s.at[g])
    wait_for(r1.at[pl.ds(1, 15)], pol_s.at[0])
    wait_for(r2.at[pl.ds(1, 15)], pol_s.at[1])
    wait_for(tw.at[pl.ds(1, 15)], tw_s.at[0])


def body(pol_cube, phasor, chan_weight, flags):
    vmem = pltpu.VMEM
    dma = pltpu.SemaphoreType.DMA
    out = pl.pallas_call(
        kernel,
        out_shape=jax.ShapeDtypeStruct((128, 2, 512), BF16),
        in_specs=[pl.BlockSpec(memory_space=pltpu.HBM)] * 4,
        out_specs=pl.BlockSpec(memory_space=vmem),
        scratch_shapes=[
            vmem((2, CH, 8, 1024), BF16),
            vmem((CH, 2, 512), BF16),
            vmem((1, CH), F32),
            vmem((8, CH), jnp.int32),
            vmem((2, 256, 128), BF16),
            vmem((CH, 8, 128), F32),
            vmem((X, Y, ROWS1, 256), BF16),
            vmem((X, Y, ROWS2, 256), BF16),
            vmem((16, ROWS1, 256), BF16),
            vmem((16, ROWS2, 256), BF16),
            vmem((2, X, Y, PH_ROWS, 128), BF16),
            vmem((16, 1, 128), F32),
            vmem((8, 256, 256), F32),
            vmem((8, 128, 256), F32),
            vmem((4, 128, 256), BF16),
            vmem((4, 128, 256), BF16),
            vmem((4, 1, 128), F32),
            dma((6,)),
            dma((2,)), dma((2,)),
            dma((8,)), dma((8,)),
            dma((1,)), dma((1,)),
            dma((8,)), dma((8,)),
            dma((4,)), dma((4,)),
            dma((2,)), dma((2,)),
            pltpu.SemaphoreType.REGULAR,
        ],
        compiler_params=pltpu.CompilerParams(
            collective_id=0, has_side_effects=True, vmem_limit_bytes=40 * 2**20
        ),
        cost_estimate=pl.CostEstimate(
            flops=2 * 512 * 1152 * 1024, bytes_accessed=2**21, transcendentals=0
        ),
        name="exchange",
    )(*[pltpu.with_memory_space_constraint(a, pltpu.HBM) for a in (pol_cube, phasor.transpose(1, 0, 2), chan_weight[None, :], flags.T)])
    return out.reshape(1, 16, 8, 2, 512)


def solution(mesh):
    placed = (P(None, "chan", None, "pix"), P(None, "chan", None), P("chan"), P("chan", None))
    return jax.shard_map(
        body,
        mesh=mesh,
        in_specs=placed,
        out_specs=P("pix", "chan", None, None, None),
        check_vma=False,
    )
```

```python
import jax
import jax.numpy as jnp
from jax import lax
from jax.experimental import pallas as pl
from jax.experimental.pallas import tpu as pltpu
from jax.sharding import PartitionSpec as P

MESH = pl.DeviceIdType.MESH
F32 = jnp.float32
BF16 = jnp.bfloat16

X, Y = 4, 4
SPREAD = [(dx, dy) for dx in (1, 3, 0, 2) for dy in range(Y) if dx or dy]
CH = 36
BODY = 32
ROWS1 = 2 * BODY + 16
ROWS2 = 2 * BODY
PH_ROWS = ROWS1 + ROWS2
POL_ROWS = 4 * BODY + 16


def tdot(a, b):
    return lax.dot_general(a, b, (((0,), (0,)), ((), ())), preferred_element_type=F32)


def kernel(
    pol_hbm, phasor_hbm, cw_hbm, flags_hbm, out,
    pol, phasor, cw, flags_t, order_o, wb, s1, s2, r1, r2, ph, tw, part, d2d, zsend, zrecv, tots,
    in_sem, pol_s, pol_r, ph_s, ph_r, tw_s, tw_r, d_s, d_r, z_s, z_r, t_s, t_r, ready,
):
    me = lax.axis_index("chan")
    pix = lax.axis_index("pix")
    core = lax.rem(me, 2)
    y = lax.rem(me // 2, Y)
    x = lax.rem(me // (2 * Y), X)
    zh = me // (2 * X * Y)

    def dev(zz, xx, yy, cc):
        return (((zz * X + xx) * Y + yy) * 2 + cc, pix)

    def plane(dx, dy):
        return dev(zh, lax.rem(x + dx, X), lax.rem(y + dy, Y), core)

    core_peer = dev(zh, x, y, 1 - core)
    z_peer = dev(1 - zh, x, y, core)
    offsets = [(dx, dy) for dx in range(X) for dy in range(Y) if dx or dy]

    barrier = pltpu.get_barrier_semaphore()
    peers = [plane(dx, dy) for dx, dy in offsets] + [core_peer]
    for target in peers:
        pl.semaphore_signal(barrier, inc=1, device_id=target, device_id_type=MESH)

    @pl.when(zh == 0)
    def _():
        pl.semaphore_signal(barrier, inc=1, device_id=z_peer, device_id_type=MESH)

    loads = [
        pltpu.make_async_copy(a, b, in_sem.at[i])
        for i, (a, b) in enumerate(
            ((flags_hbm, flags_t), (cw_hbm, cw), (phasor_hbm, phasor), (pol_hbm, pol))
        )
    ]
    for c in loads:
        c.start()

    i = lax.broadcasted_iota(jnp.int32, (256, 256), 0)
    j = lax.broadcasted_iota(jnp.int32, (256, 256), 1)
    order = jnp.where((i % 32) * 8 + i // 32 == j, 1.0, 0.0).astype(BF16)
    i, j = i[:64, :64], j[:64, :64]
    order_t = jnp.where((i % 8) * 8 + i // 8 == j, 1.0, 0.0).astype(BF16)

    i = lax.broadcasted_iota(jnp.int32, (256, 128), 0)
    j = lax.broadcasted_iota(jnp.int32, (256, 128), 1)
    at_row = (i // 2) % 8 * 16 + i // 16 == j
    for k in range(2):
        order_o[k] = jnp.where(at_row & (i % 2 == k), 1.0, 0.0).astype(BF16)

    loads[0].wait()
    loads[1].wait()
    w = cw[...] * flags_t[...].astype(F32)
    for c in range(CH):
        wb[c] = jnp.broadcast_to(w[:, c : c + 1], (8, 128))
    row_sum = jnp.sum(w, axis=1, keepdims=True)
    lane = lax.broadcasted_iota(jnp.int32, (8, 128), 1)
    sub = lax.broadcasted_iota(jnp.int32, (8, 128), 0)
    tw[0] = jnp.sum(jnp.where(lane // 16 == sub, row_sum, 0.0), axis=0, keepdims=True)

    loads[2].wait()
    both = phasor[...].astype(F32)
    re, im = both[:, 0], both[:, 1]
    tails = [jnp.concatenate([re[BODY:, h : h + 256], -im[BODY:, h : h + 256]], axis=0) for h in (0, 256)]
    block = jnp.concatenate(
        [re[:BODY, :256], im[:BODY, :256]] + tails + [re[:BODY, 256:], im[:BODY, 256:]], axis=0
    ).astype(BF16)
    ph[0, 0, 0] = block[:, :128]
    ph[1, 0, 0] = block[:, 128:]

    lane_b = lax.broadcasted_iota(jnp.int32, (1, 128), 1)

    def swap_blocks(v):
        for k in range(3):
            m = 1 << k
            mask = jnp.broadcast_to((lane_b // (16 * m)) % 2 == 1, v[0].shape)
            new = list(v)
            for a in range(8):
                if a & m:
                    continue
                b = a | m
                new[a] = jnp.where(mask, pltpu.roll(v[b], 16 * m, 1), v[a])
                new[b] = jnp.where(mask, v[b], pltpu.roll(v[a], 128 - 16 * m, 1))
            v = new
        return v

    def weighted(s, chans, at):
        v = pol[s, chans, :, pl.ds(at, 128)].astype(F32) * wb[chans]
        return v.reshape(-1, 128).astype(BF16)

    def regroup(matrix, v, rows, kind):
        u = jnp.dot(matrix, v, preferred_element_type=F32).astype(kind)
        return swap_blocks([u[r * rows : (r + 1) * rows] for r in range(8)])

    def relayout(first, dx):
        xx = lax.rem(x + dx, X)
        at = pl.multiple_of(((1 - zh if first else zh) * X + xx) * 128, 128)
        dst = s1 if first else s2
        for s in range(2):
            v = regroup(order, weighted(s, slice(0, BODY), at), BODY, BF16)
            for g in range(8):
                dst[dx, g // 2, pl.ds((g % 2) * 2 * BODY + s * BODY, BODY), :] = v[g]
        v = [weighted(s, slice(BODY, CH), at) for s in range(2)]
        v = regroup(order_t, jnp.concatenate(v, axis=0), 8, F32)
        for yy in range(Y):
            tail = jnp.concatenate([v[2 * yy], v[2 * yy + 1]], axis=0)
            dst[dx, yy, pl.ds(4 * BODY, 16), :] = tail.astype(BF16)

    loads[3].wait()
    near_x = (1, 3, 0, 2)
    for dx in near_x:
        relayout(True, dx)

    pl.semaphore_wait(barrier, len(peers) + zh)

    @pl.when(zh == 1)
    def _():
        pl.semaphore_signal(ready, inc=1, device_id=z_peer, device_id_type=MESH)

    def rcopy(src, dst, ss, rs, target):
        return pltpu.make_async_remote_copy(
            src_ref=src, dst_ref=dst, send_sem=ss, recv_sem=rs,
            device_id=target, device_id_type=MESH,
        )

    def wait_for(view, sem):
        pltpu.make_async_copy(view, view, sem).wait()

    ring = (1, 3, 2)
    rest = pl.ds(1, 3)
    rows_a, rows_b = pl.ds(0, ROWS1), pl.ds(ROWS1, ROWS2)
    arrive = [
        ph.at[0, rest, 0],
        ph.at[1, 0, rest],
        ph.at[0, 0, rest],
        ph.at[1, rest, 0],
        ph.at[0, rest, rest, rows_a],
        ph.at[1, rest, rest, rows_a],
        ph.at[0, rest, rest, rows_b],
        ph.at[1, rest, rest, rows_b],
    ]
    for d in ring:
        rcopy(ph.at[0, 0, 0], ph.at[0, d, 0], ph_s.at[0], ph_r.at[0], plane(d, 0)).start()
        rcopy(ph.at[1, 0, 0], ph.at[1, 0, d], ph_s.at[1], ph_r.at[1], plane(0, d)).start()
    for d in ring:
        rcopy(ph.at[0, 0, 0], ph.at[0, 0, d], ph_s.at[2], ph_r.at[2], plane(0, d)).start()
        rcopy(ph.at[1, 0, 0], ph.at[1, d, 0], ph_s.at[3], ph_r.at[3], plane(d, 0)).start()

    def send_pol(first, dx, dy):
        q = 0 if first else 1
        src, dst = (s1, r1) if first else (s2, r2)
        rcopy(
            src.at[dx, lax.rem(y + dy, Y)], dst.at[dx * 4 + dy],
            pol_s.at[q], pol_r.at[q], plane(dx, dy),
        ).start()

    pltpu.make_async_copy(s1.at[0, y], r1.at[0], in_sem.at[4]).start()
    for dx, dy in offsets:
        k = dx * 4 + dy
        rcopy(tw.at[0], tw.at[k], tw_s.at[0], tw_r.at[0], plane(dx, dy)).start()

    for dx, dy in SPREAD:
        send_pol(True, dx, dy)

    def forward(q, strip, rows):
        for d in ring:
            if strip == 0:
                c = rcopy(
                    ph.at[0, rest, 0, rows], ph.at[0, rest, d, rows],
                    ph_s.at[q], ph_r.at[q], plane(0, d),
                )
            else:
                c = rcopy(
                    ph.at[1, 0, rest, rows], ph.at[1, d, rest, rows],
                    ph_s.at[q], ph_r.at[q], plane(d, 0),
                )
            c.start()

    wait_for(arrive[0], ph_r.at[0])
    forward(4, 0, rows_a)
    wait_for(arrive[1], ph_r.at[1])
    forward(5, 1, rows_a)
    forward(6, 0, rows_b)
    forward(7, 1, rows_b)

    for dx in near_x:
        relayout(False, dx)
    pltpu.make_async_copy(s2.at[0, y], r2.at[0], in_sem.at[5]).start()

    wait_for(tw.at[pl.ds(1, 15)], tw_r.at[0])
    tots[0] = jnp.sum(tw[...], axis=0)
    ct = rcopy(tots.at[0], tots.at[1], t_s.at[0], t_r.at[0], core_peer)
    ct.start()

    def contract(first, half):
        src = r1 if first else r2
        at = 0 if half == 0 else ROWS1
        def columns(lo):
            return jnp.concatenate(
                [src[:, at : at + BODY].reshape(16 * BODY, 128) for at in (lo, lo + 2 * BODY)],
                axis=1,
            )

        w0, w1 = columns(0), columns(BODY)
        lt = src[:, 4 * BODY :].astype(F32)
        lt = jnp.concatenate([lt[:, :8].reshape(128, 128), lt[:, 8:].reshape(128, 128)], axis=1)
        lt = lt.astype(BF16)

        def lanes(lo, hi):
            return jnp.concatenate(
                [ph[s, :, :, lo:hi].reshape(-1, 128) for s in range(2)], axis=1
            )

        pr = lanes(at, at + BODY)
        pi = lanes(at + BODY, at + 2 * BODY)
        pt = lanes(2 * BODY, ROWS1).reshape(16, 16, 256).astype(F32)
        pt = pt[:, :8] if half == 0 else pt[:, 8:]
        turned = jnp.concatenate([-pt[:, 4:], pt[:, :4]], axis=1)
        pt = pt.reshape(128, 256).astype(BF16)
        turned = turned.reshape(128, 256).astype(BF16)
        yield tdot(w0, pr) - tdot(w1, pi) + tdot(lt, pt)
        yield tdot(w0, pi) + tdot(w1, pr) + tdot(lt, turned)

    mine = pl.multiple_of(core * 128, 128)
    theirs = pl.multiple_of((1 - core) * 128, 128)

    def spread(first, half):
        copies = []
        for k, value in enumerate(contract(first, half)):
            n = (0 if first else 4) + half * 2 + k
            part[n] = value
            c = rcopy(part.at[n, pl.ds(theirs, 128)], d2d.at[n], d_s.at[n], d_r.at[n], core_peer)
            c.start()
            copies.append(c)
        return copies

    d_copies, z_copies = [], []
    for g in (2, 3, 4, 5):
        wait_for(arrive[g], ph_r.at[g])
    for dx, dy in SPREAD:
        send_pol(False, dx, dy)
    wait_for(r1.at[pl.ds(1, 15)], pol_r.at[0])
    wait_for(r1.at[0], in_sem.at[4])
    @pl.when(zh == 0)
    def _():
        pl.semaphore_wait(ready, 1)

    for half in range(2):
        if half == 1:
            for g in (6, 7):
                wait_for(arrive[g], ph_r.at[g])
        d_copies += spread(True, half)
        if half == 0:
            ct.wait_recv()
            tots[2] = tots[0] + tots[1]
            cz = rcopy(tots.at[2], tots.at[3], t_s.at[1], t_r.at[1], z_peer)
            cz.start()
        for n in (half * 2, half * 2 + 1):
            d_copies[n].wait_recv()
            zsend[n] = (part[n, pl.ds(mine, 128)] + d2d[n]).astype(BF16)
            c = rcopy(zsend.at[n], zrecv.at[n], z_s.at[n], z_r.at[n], z_peer)
            c.start()
            z_copies.append(c)

    wait_for(r2.at[pl.ds(1, 15)], pol_r.at[1])
    wait_for(r2.at[0], in_sem.at[5])
    d_copies += spread(False, 0) + spread(False, 1)
    cz.wait_recv()
    total = tots[2] + tots[3]
    ri = lax.broadcasted_iota(jnp.int32, (128, 128), 0)
    ci = lax.broadcasted_iota(jnp.int32, (128, 128), 1)
    column = jnp.sum(jnp.where(ri == ci, total, 0.0), axis=1, keepdims=True)
    for half in range(2):
        rows = 0.0
        for k in range(2):
            n = half * 2 + k
            z_copies[n].wait_recv()
            d_copies[4 + n].wait_recv()
            summed = part[4 + n, pl.ds(mine, 128)] + d2d[4 + n] + zrecv[n].astype(F32)
            value = (summed / column).astype(BF16)
            rows = rows + jnp.dot(order_o[k], value, preferred_element_type=F32)
        out[:, :, pl.ds(half * 256, 256)] = rows.astype(BF16).reshape(128, 2, 256)

    for c in [ct, cz] + d_copies + z_copies:
        c.wait_send()
    for g in range(8):
        wait_for(arrive[g], ph_s.at[g])
    wait_for(r1.at[pl.ds(1, 15)], pol_s.at[0])
    wait_for(r2.at[pl.ds(1, 15)], pol_s.at[1])
    wait_for(tw.at[pl.ds(1, 15)], tw_s.at[0])


def body(pol_cube, phasor, chan_weight, flags):
    vmem = pltpu.VMEM
    dma = pltpu.SemaphoreType.DMA
    out = pl.pallas_call(
        kernel,
        out_shape=jax.ShapeDtypeStruct((128, 2, 512), BF16),
        in_specs=[pl.BlockSpec(memory_space=pltpu.HBM)] * 4,
        out_specs=pl.BlockSpec(memory_space=vmem),
        scratch_shapes=[
            vmem((2, CH, 8, 1024), BF16),
            vmem((CH, 2, 512), BF16),
            vmem((1, CH), F32),
            vmem((8, CH), jnp.int32),
            vmem((2, 256, 128), BF16),
            vmem((CH, 8, 128), F32),
            vmem((X, Y, POL_ROWS, 128), BF16),
            vmem((X, Y, POL_ROWS, 128), BF16),
            vmem((16, POL_ROWS, 128), BF16),
            vmem((16, POL_ROWS, 128), BF16),
            vmem((2, X, Y, PH_ROWS, 128), BF16),
            vmem((16, 1, 128), F32),
            vmem((8, 256, 256), F32),
            vmem((8, 128, 256), F32),
            vmem((4, 128, 256), BF16),
            vmem((4, 128, 256), BF16),
            vmem((4, 1, 128), F32),
            dma((6,)),
            dma((2,)), dma((2,)),
            dma((8,)), dma((8,)),
            dma((1,)), dma((1,)),
            dma((8,)), dma((8,)),
            dma((4,)), dma((4,)),
            dma((2,)), dma((2,)),
            pltpu.SemaphoreType.REGULAR,
        ],
        compiler_params=pltpu.CompilerParams(
            collective_id=0, has_side_effects=True, vmem_limit_bytes=40 * 2**20
        ),
        cost_estimate=pl.CostEstimate(
            flops=2 * 512 * 1152 * 1024, bytes_accessed=2**21, transcendentals=0
        ),
        name="exchange",
    )(*[pltpu.with_memory_space_constraint(a, pltpu.HBM) for a in (pol_cube, phasor.transpose(1, 0, 2), chan_weight[None, :], flags.T)])
    return out.reshape(1, 16, 8, 2, 512)


def solution(mesh):
    placed = (P(None, "chan", None, "pix"), P(None, "chan", None), P("chan"), P("chan", None))
    return jax.shard_map(
        body,
        mesh=mesh,
        in_specs=placed,
        out_specs=P("pix", "chan", None, None, None),
        check_vma=False,
    )
```

```python
import jax
import jax.numpy as jnp
from jax import lax
from jax.experimental import pallas as pl
from jax.experimental.pallas import tpu as pltpu
from jax.sharding import PartitionSpec as P

MESH = pl.DeviceIdType.MESH
F32 = jnp.float32
BF16 = jnp.bfloat16

X, Y = 4, 4
SPREAD = [(dx, dy) for dx in (1, 3, 0, 2) for dy in range(Y) if dx or dy]
CH = 36
BODY = 32
ROWS1 = 2 * BODY + 16
ROWS2 = 2 * BODY
PH_ROWS = ROWS1 + ROWS2
POL_ROWS = 4 * BODY + 16


def tdot(a, b):
    return lax.dot_general(a, b, (((0,), (0,)), ((), ())), preferred_element_type=F32)


def kernel(
    pol_hbm, phasor_hbm, cw_hbm, flags_hbm, out,
    pol, phasor, cw, flags_t, order_o, wb, s1, s2, r1, r2, ph, tw, part, d2d, zsend, zrecv, tots,
    in_sem, pol_s, pol_r, ph_s, ph_r, tw_s, tw_r, d_s, d_r, z_s, z_r, t_s, t_r, ready,
):
    me = lax.axis_index("chan")
    pix = lax.axis_index("pix")
    core = lax.rem(me, 2)
    y = lax.rem(me // 2, Y)
    x = lax.rem(me // (2 * Y), X)
    zh = me // (2 * X * Y)

    def dev(zz, xx, yy, cc):
        return (((zz * X + xx) * Y + yy) * 2 + cc, pix)

    def plane(dx, dy):
        return dev(zh, lax.rem(x + dx, X), lax.rem(y + dy, Y), core)

    core_peer = dev(zh, x, y, 1 - core)
    z_peer = dev(1 - zh, x, y, core)
    offsets = [(dx, dy) for dx in range(X) for dy in range(Y) if dx or dy]

    barrier = pltpu.get_barrier_semaphore()
    peers = [plane(dx, dy) for dx, dy in offsets] + [core_peer]
    for target in peers:
        pl.semaphore_signal(barrier, inc=1, device_id=target, device_id_type=MESH)

    @pl.when(zh == 0)
    def _():
        pl.semaphore_signal(barrier, inc=1, device_id=z_peer, device_id_type=MESH)

    loads = [
        pltpu.make_async_copy(a, b, in_sem.at[i])
        for i, (a, b) in enumerate(
            ((flags_hbm, flags_t), (cw_hbm, cw), (phasor_hbm, phasor), (pol_hbm, pol))
        )
    ]
    for c in loads:
        c.start()

    i = lax.broadcasted_iota(jnp.int32, (256, 256), 0)
    j = lax.broadcasted_iota(jnp.int32, (256, 256), 1)
    order = jnp.where((i % 32) * 8 + i // 32 == j, 1.0, 0.0).astype(BF16)
    i, j = i[:64, :64], j[:64, :64]
    order_t = jnp.where((i % 8) * 8 + i // 8 == j, 1.0, 0.0).astype(BF16)

    i = lax.broadcasted_iota(jnp.int32, (256, 128), 0)
    j = lax.broadcasted_iota(jnp.int32, (256, 128), 1)
    at_row = (i // 2) % 8 * 16 + i // 16 == j
    for k in range(2):
        order_o[k] = jnp.where(at_row & (i % 2 == k), 1.0, 0.0).astype(BF16)

    loads[0].wait()
    loads[1].wait()
    w = cw[...] * flags_t[...].astype(F32)
    for c in range(CH):
        wb[c] = jnp.broadcast_to(w[:, c : c + 1], (8, 128))
    row_sum = jnp.sum(w, axis=1, keepdims=True)
    lane = lax.broadcasted_iota(jnp.int32, (8, 128), 1)
    sub = lax.broadcasted_iota(jnp.int32, (8, 128), 0)
    tw[0] = jnp.sum(jnp.where(lane // 16 == sub, row_sum, 0.0), axis=0, keepdims=True)

    loads[2].wait()
    both = phasor[...].astype(F32)
    re, im = both[:, 0], both[:, 1]
    tails = [jnp.concatenate([re[BODY:, h : h + 256], -im[BODY:, h : h + 256]], axis=0) for h in (0, 256)]
    block = jnp.concatenate(
        [re[:BODY, :256], im[:BODY, :256]] + tails + [re[:BODY, 256:], im[:BODY, 256:]], axis=0
    ).astype(BF16)
    ph[0, 0, 0] = block[:, :128]
    ph[1, 0, 0] = block[:, 128:]

    lane_b = lax.broadcasted_iota(jnp.int32, (1, 128), 1)

    def swap_blocks(v):
        for k in range(3):
            m = 1 << k
            mask = jnp.broadcast_to((lane_b // (16 * m)) % 2 == 1, v[0].shape)
            new = list(v)
            for a in range(8):
                if a & m:
                    continue
                b = a | m
                new[a] = jnp.where(mask, pltpu.roll(v[b], 16 * m, 1), v[a])
                new[b] = jnp.where(mask, v[b], pltpu.roll(v[a], 128 - 16 * m, 1))
            v = new
        return v

    def weighted(s, chans, at):
        v = pol[s, chans, :, pl.ds(at, 128)].astype(F32) * wb[chans]
        return v.reshape(-1, 128).astype(BF16)

    def regroup(matrix, v, rows, kind):
        u = jnp.dot(matrix, v, preferred_element_type=F32).astype(kind)
        return swap_blocks([u[r * rows : (r + 1) * rows] for r in range(8)])

    def relayout(first, dx):
        xx = lax.rem(x + dx, X)
        at = pl.multiple_of(((1 - zh if first else zh) * X + xx) * 128, 128)
        dst = s1 if first else s2
        for s in range(2):
            v = regroup(order, weighted(s, slice(0, BODY), at), BODY, BF16)
            for g in range(8):
                dst[dx, g // 2, pl.ds((g % 2) * 2 * BODY + s * BODY, BODY), :] = v[g]
        v = [weighted(s, slice(BODY, CH), at) for s in range(2)]
        v = regroup(order_t, jnp.concatenate(v, axis=0), 8, F32)
        for yy in range(Y):
            tail = jnp.concatenate([v[2 * yy], v[2 * yy + 1]], axis=0)
            dst[dx, yy, pl.ds(4 * BODY, 16), :] = tail.astype(BF16)

    loads[3].wait()
    near_x = (1, 3, 0, 2)
    for dx in near_x:
        relayout(True, dx)

    pl.semaphore_wait(barrier, len(peers) + zh)

    @pl.when(zh == 1)
    def _():
        pl.semaphore_signal(ready, inc=1, device_id=z_peer, device_id_type=MESH)

    def rcopy(src, dst, ss, rs, target):
        return pltpu.make_async_remote_copy(
            src_ref=src, dst_ref=dst, send_sem=ss, recv_sem=rs,
            device_id=target, device_id_type=MESH,
        )

    def wait_for(view, sem):
        pltpu.make_async_copy(view, view, sem).wait()

    ring = (2, 1, 3)
    rest = pl.ds(1, 3)
    rows_a, rows_b = pl.ds(0, ROWS1), pl.ds(ROWS1, ROWS2)
    arrive = [
        ph.at[0, rest, 0],
        ph.at[1, 0, rest],
        ph.at[0, 0, rest],
        ph.at[1, rest, 0],
        ph.at[0, rest, rest, rows_a],
        ph.at[1, rest, rest, rows_a],
        ph.at[0, rest, rest, rows_b],
        ph.at[1, rest, rest, rows_b],
    ]
    for d in ring:
        rcopy(ph.at[0, 0, 0], ph.at[0, d, 0], ph_s.at[0], ph_r.at[0], plane(d, 0)).start()
        rcopy(ph.at[1, 0, 0], ph.at[1, 0, d], ph_s.at[1], ph_r.at[1], plane(0, d)).start()
    for d in ring:
        rcopy(ph.at[0, 0, 0], ph.at[0, 0, d], ph_s.at[2], ph_r.at[2], plane(0, d)).start()
        rcopy(ph.at[1, 0, 0], ph.at[1, d, 0], ph_s.at[3], ph_r.at[3], plane(d, 0)).start()

    def send_pol(first, dx, dy):
        q = 0 if first else 1 + dx
        src, dst = (s1, r1) if first else (s2, r2)
        rcopy(
            src.at[dx, lax.rem(y + dy, Y)], dst.at[dx * 4 + dy],
            pol_s.at[q], pol_r.at[q], plane(dx, dy),
        ).start()

    pltpu.make_async_copy(s1.at[0, y], r1.at[0], in_sem.at[4]).start()
    for dx, dy in offsets:
        k = dx * 4 + dy
        rcopy(tw.at[0], tw.at[k], tw_s.at[0], tw_r.at[0], plane(dx, dy)).start()

    for dx, dy in SPREAD:
        send_pol(True, dx, dy)

    def forward(q, strip, rows):
        for d in ring:
            if strip == 0:
                c = rcopy(
                    ph.at[0, rest, 0, rows], ph.at[0, rest, d, rows],
                    ph_s.at[q], ph_r.at[q], plane(0, d),
                )
            else:
                c = rcopy(
                    ph.at[1, 0, rest, rows], ph.at[1, d, rest, rows],
                    ph_s.at[q], ph_r.at[q], plane(d, 0),
                )
            c.start()

    wait_for(arrive[0], ph_r.at[0])
    forward(4, 0, rows_a)
    wait_for(arrive[1], ph_r.at[1])
    forward(5, 1, rows_a)
    forward(6, 0, rows_b)
    forward(7, 1, rows_b)

    for dx in near_x:
        relayout(False, dx)
    pltpu.make_async_copy(s2.at[0, y], r2.at[0], in_sem.at[5]).start()

    wait_for(tw.at[pl.ds(1, 15)], tw_r.at[0])
    tots[0] = jnp.sum(tw[...], axis=0)
    ct = rcopy(tots.at[0], tots.at[1], t_s.at[0], t_r.at[0], core_peer)
    ct.start()

    def contract(first, half, xs):
        src = r1 if first else r2
        at = 0 if half == 0 else ROWS1
        def taken(ref, rows):
            return jnp.concatenate(
                [ref[4 * dx : 4 * dx + 4, rows].reshape(-1, 128) for dx in xs], axis=0
            )

        def columns(lo):
            return jnp.concatenate(
                [taken(src, slice(c, c + BODY)) for c in (lo, lo + 2 * BODY)], axis=1
            )

        w0, w1 = columns(0), columns(BODY)
        count = 4 * len(xs)
        lt = taken(src, slice(4 * BODY, POL_ROWS)).astype(F32).reshape(count, 16, 128)
        lt = jnp.concatenate([lt[:, :8].reshape(-1, 128), lt[:, 8:].reshape(-1, 128)], axis=1)
        lt = lt.astype(BF16)

        def lanes(lo, hi):
            return jnp.concatenate(
                [
                    jnp.concatenate([ph[s, dx, :, lo:hi].reshape(-1, 128) for dx in xs], axis=0)
                    for s in range(2)
                ],
                axis=1,
            )

        pr = lanes(at, at + BODY)
        pi = lanes(at + BODY, at + 2 * BODY)
        pt = lanes(2 * BODY, ROWS1).reshape(count, 16, 256).astype(F32)
        pt = pt[:, :8] if half == 0 else pt[:, 8:]
        turned = jnp.concatenate([-pt[:, 4:], pt[:, :4]], axis=1)
        pt = pt.reshape(-1, 256).astype(BF16)
        turned = turned.reshape(-1, 256).astype(BF16)
        yield tdot(w0, pr) - tdot(w1, pi) + tdot(lt, pt)
        yield tdot(w0, pi) + tdot(w1, pr) + tdot(lt, turned)

    mine = pl.multiple_of(core * 128, 128)
    theirs = pl.multiple_of((1 - core) * 128, 128)

    def spread(first, half):
        copies = []
        for k, value in enumerate(contract(first, half, range(X) if first else (0, 2))):
            n = (0 if first else 4) + half * 2 + k
            part[n] = value if first else part[n] + value
            c = rcopy(part.at[n, pl.ds(theirs, 128)], d2d.at[n], d_s.at[n], d_r.at[n], core_peer)
            c.start()
            copies.append(c)
        return copies

    d_copies, z_copies = [], []
    for g in (2, 3, 4, 5):
        wait_for(arrive[g], ph_r.at[g])
    for dx, dy in SPREAD:
        send_pol(False, dx, dy)
    wait_for(r1.at[pl.ds(1, 15)], pol_r.at[0])
    wait_for(r1.at[0], in_sem.at[4])
    @pl.when(zh == 0)
    def _():
        pl.semaphore_wait(ready, 1)

    for half in range(2):
        if half == 1:
            for g in (6, 7):
                wait_for(arrive[g], ph_r.at[g])
        d_copies += spread(True, half)
        if half == 0:
            ct.wait_recv()
            tots[2] = tots[0] + tots[1]
            cz = rcopy(tots.at[2], tots.at[3], t_s.at[1], t_r.at[1], z_peer)
            cz.start()
        for n in (half * 2, half * 2 + 1):
            d_copies[n].wait_recv()
            zsend[n] = (part[n, pl.ds(mine, 128)] + d2d[n]).astype(BF16)
            c = rcopy(zsend.at[n], zrecv.at[n], z_s.at[n], z_r.at[n], z_peer)
            c.start()
            z_copies.append(c)

    own_slots = [pl.ds(1, 3)] + [pl.ds(4 * dx, 4) for dx in range(1, X)]
    for dx in (1, 3):
        wait_for(r2.at[own_slots[dx]], pol_r.at[1 + dx])
    for half in range(2):
        for k, value in enumerate(contract(False, half, (1, 3))):
            part[4 + half * 2 + k] = value
    for dx in (0, 2):
        wait_for(r2.at[own_slots[dx]], pol_r.at[1 + dx])
    wait_for(r2.at[0], in_sem.at[5])
    d_copies += spread(False, 0) + spread(False, 1)
    cz.wait_recv()
    total = tots[2] + tots[3]
    ri = lax.broadcasted_iota(jnp.int32, (128, 128), 0)
    ci = lax.broadcasted_iota(jnp.int32, (128, 128), 1)
    column = jnp.sum(jnp.where(ri == ci, total, 0.0), axis=1, keepdims=True)
    for half in range(2):
        rows = 0.0
        for k in range(2):
            n = half * 2 + k
            z_copies[n].wait_recv()
            d_copies[4 + n].wait_recv()
            summed = part[4 + n, pl.ds(mine, 128)] + d2d[4 + n] + zrecv[n].astype(F32)
            value = (summed / column).astype(BF16)
            rows = rows + jnp.dot(order_o[k], value, preferred_element_type=F32)
        out[:, :, pl.ds(half * 256, 256)] = rows.astype(BF16).reshape(128, 2, 256)

    for c in [ct, cz] + d_copies + z_copies:
        c.wait_send()
    for g in range(8):
        wait_for(arrive[g], ph_s.at[g])
    wait_for(r1.at[pl.ds(1, 15)], pol_s.at[0])
    for dx in range(X):
        wait_for(r2.at[own_slots[dx]], pol_s.at[1 + dx])
    wait_for(tw.at[pl.ds(1, 15)], tw_s.at[0])


def body(pol_cube, phasor, chan_weight, flags):
    vmem = pltpu.VMEM
    dma = pltpu.SemaphoreType.DMA
    out = pl.pallas_call(
        kernel,
        out_shape=jax.ShapeDtypeStruct((128, 2, 512), BF16),
        in_specs=[pl.BlockSpec(memory_space=pltpu.HBM)] * 4,
        out_specs=pl.BlockSpec(memory_space=vmem),
        scratch_shapes=[
            vmem((2, CH, 8, 1024), BF16),
            vmem((CH, 2, 512), BF16),
            vmem((1, CH), F32),
            vmem((8, CH), jnp.int32),
            vmem((2, 256, 128), BF16),
            vmem((CH, 8, 128), F32),
            vmem((X, Y, POL_ROWS, 128), BF16),
            vmem((X, Y, POL_ROWS, 128), BF16),
            vmem((16, POL_ROWS, 128), BF16),
            vmem((16, POL_ROWS, 128), BF16),
            vmem((2, X, Y, PH_ROWS, 128), BF16),
            vmem((16, 1, 128), F32),
            vmem((8, 256, 256), F32),
            vmem((8, 128, 256), F32),
            vmem((4, 128, 256), BF16),
            vmem((4, 128, 256), BF16),
            vmem((4, 1, 128), F32),
            dma((6,)),
            dma((5,)), dma((5,)),
            dma((8,)), dma((8,)),
            dma((1,)), dma((1,)),
            dma((8,)), dma((8,)),
            dma((4,)), dma((4,)),
            dma((2,)), dma((2,)),
            pltpu.SemaphoreType.REGULAR,
        ],
        compiler_params=pltpu.CompilerParams(
            collective_id=0, has_side_effects=True, vmem_limit_bytes=40 * 2**20
        ),
        cost_estimate=pl.CostEstimate(
            flops=2 * 512 * 1152 * 1024, bytes_accessed=2**21, transcendentals=0
        ),
        name="exchange",
    )(*[pltpu.with_memory_space_constraint(a, pltpu.HBM) for a in (pol_cube, phasor.transpose(1, 0, 2), chan_weight[None, :], flags.T)])
    return out.reshape(1, 16, 8, 2, 512)


def solution(mesh):
    placed = (P(None, "chan", None, "pix"), P(None, "chan", None), P("chan"), P("chan", None))
    return jax.shard_map(
        body,
        mesh=mesh,
        in_specs=placed,
        out_specs=P("pix", "chan", None, None, None),
        check_vma=False,
    )
```

```python
import jax
import jax.numpy as jnp
from jax import lax
from jax.experimental import pallas as pl
from jax.experimental.pallas import tpu as pltpu
from jax.sharding import PartitionSpec as P

MESH = pl.DeviceIdType.MESH
F32 = jnp.float32
BF16 = jnp.bfloat16

X, Y = 4, 4
SPREAD = [(dx, dy) for dx in (1, 3, 0, 2) for dy in range(Y) if dx or dy]
CH = 36
BODY = 32
ROWS1 = 2 * BODY + 16
ROWS2 = 2 * BODY
PH_ROWS = ROWS1 + ROWS2
POL_ROWS = 4 * BODY + 16


def tdot(a, b):
    return lax.dot_general(a, b, (((0,), (0,)), ((), ())), preferred_element_type=F32)


def kernel(
    pol_hbm, phasor_hbm, cw_hbm, flags_hbm, out,
    pol, phasor, cw, flags_t, order_o, wb, s1, s2, r1, r2, ph, tw, part, d2d, zsend, zrecv, tots,
    in_sem, pol_s, pol_r, ph_s, ph_r, tw_s, tw_r, d_s, d_r, z_s, z_r, t_s, t_r, ready,
):
    me = lax.axis_index("chan")
    pix = lax.axis_index("pix")
    core = lax.rem(me, 2)
    y = lax.rem(me // 2, Y)
    x = lax.rem(me // (2 * Y), X)
    zh = me // (2 * X * Y)

    def dev(zz, xx, yy, cc):
        return (((zz * X + xx) * Y + yy) * 2 + cc, pix)

    def plane(dx, dy):
        return dev(zh, lax.rem(x + dx, X), lax.rem(y + dy, Y), core)

    core_peer = dev(zh, x, y, 1 - core)
    z_peer = dev(1 - zh, x, y, core)
    offsets = [(dx, dy) for dx in range(X) for dy in range(Y) if dx or dy]

    barrier = pltpu.get_barrier_semaphore()
    peers = [plane(dx, dy) for dx, dy in offsets] + [core_peer]
    for target in peers:
        pl.semaphore_signal(barrier, inc=1, device_id=target, device_id_type=MESH)

    @pl.when(zh == 0)
    def _():
        pl.semaphore_signal(barrier, inc=1, device_id=z_peer, device_id_type=MESH)

    loads = [
        pltpu.make_async_copy(a, b, in_sem.at[i])
        for i, (a, b) in enumerate(
            ((flags_hbm, flags_t), (cw_hbm, cw), (phasor_hbm, phasor), (pol_hbm, pol))
        )
    ]
    for c in loads:
        c.start()

    i = lax.broadcasted_iota(jnp.int32, (256, 256), 0)
    j = lax.broadcasted_iota(jnp.int32, (256, 256), 1)
    order = jnp.where((i % 32) * 8 + i // 32 == j, 1.0, 0.0).astype(BF16)
    i, j = i[:64, :64], j[:64, :64]
    order_t = jnp.where((i % 8) * 8 + i // 8 == j, 1.0, 0.0).astype(BF16)

    i = lax.broadcasted_iota(jnp.int32, (256, 128), 0)
    j = lax.broadcasted_iota(jnp.int32, (256, 128), 1)
    at_row = (i // 2) % 8 * 16 + i // 16 == j
    for k in range(2):
        order_o[k] = jnp.where(at_row & (i % 2 == k), 1.0, 0.0).astype(BF16)

    loads[0].wait()
    loads[1].wait()
    w = cw[...] * flags_t[...].astype(F32)
    for c in range(CH):
        wb[c] = jnp.broadcast_to(w[:, c : c + 1], (8, 128))
    row_sum = jnp.sum(w, axis=1, keepdims=True)
    lane = lax.broadcasted_iota(jnp.int32, (8, 128), 1)
    sub = lax.broadcasted_iota(jnp.int32, (8, 128), 0)
    tw[0] = jnp.sum(jnp.where(lane // 16 == sub, row_sum, 0.0), axis=0, keepdims=True)

    loads[2].wait()
    both = phasor[...].astype(F32)
    re, im = both[:, 0], both[:, 1]
    tails = [jnp.concatenate([re[BODY:, h : h + 256], -im[BODY:, h : h + 256]], axis=0) for h in (0, 256)]
    block = jnp.concatenate(
        [re[:BODY, :256], im[:BODY, :256]] + tails + [re[:BODY, 256:], im[:BODY, 256:]], axis=0
    ).astype(BF16)
    ph[0, 0, 0] = block[:, :128]
    ph[1, 0, 0] = block[:, 128:]

    lane_b = lax.broadcasted_iota(jnp.int32, (1, 128), 1)

    def swap_blocks(v):
        for k in range(3):
            m = 1 << k
            mask = jnp.broadcast_to((lane_b // (16 * m)) % 2 == 1, v[0].shape)
            new = list(v)
            for a in range(8):
                if a & m:
                    continue
                b = a | m
                new[a] = jnp.where(mask, pltpu.roll(v[b], 16 * m, 1), v[a])
                new[b] = jnp.where(mask, v[b], pltpu.roll(v[a], 128 - 16 * m, 1))
            v = new
        return v

    def weighted(s, chans, at):
        v = pol[s, chans, :, pl.ds(at, 128)].astype(F32) * wb[chans]
        return v.reshape(-1, 128).astype(BF16)

    def regroup(matrix, v, rows, kind):
        u = jnp.dot(matrix, v, preferred_element_type=F32).astype(kind)
        return swap_blocks([u[r * rows : (r + 1) * rows] for r in range(8)])

    def relayout(first, dx):
        xx = lax.rem(x + dx, X)
        at = pl.multiple_of(((1 - zh if first else zh) * X + xx) * 128, 128)
        dst = s1 if first else s2
        for s in range(2):
            v = regroup(order, weighted(s, slice(0, BODY), at), BODY, BF16)
            for g in range(8):
                dst[dx, g // 2, pl.ds((g % 2) * 2 * BODY + s * BODY, BODY), :] = v[g]
        v = [weighted(s, slice(BODY, CH), at) for s in range(2)]
        v = regroup(order_t, jnp.concatenate(v, axis=0), 8, F32)
        for yy in range(Y):
            tail = jnp.concatenate([v[2 * yy], v[2 * yy + 1]], axis=0)
            dst[dx, yy, pl.ds(4 * BODY, 16), :] = tail.astype(BF16)

    loads[3].wait()
    near_x = (1, 3, 0, 2)
    for dx in near_x:
        relayout(True, dx)

    pl.semaphore_wait(barrier, len(peers) + zh)

    @pl.when(zh == 1)
    def _():
        pl.semaphore_signal(ready, inc=1, device_id=z_peer, device_id_type=MESH)

    def rcopy(src, dst, ss, rs, target):
        return pltpu.make_async_remote_copy(
            src_ref=src, dst_ref=dst, send_sem=ss, recv_sem=rs,
            device_id=target, device_id_type=MESH,
        )

    def wait_for(view, sem):
        pltpu.make_async_copy(view, view, sem).wait()

    ring = (2, 1, 3)
    rest = pl.ds(1, 3)
    rows_a, rows_b = pl.ds(0, ROWS1), pl.ds(ROWS1, ROWS2)
    arrive = [
        ph.at[0, rest, 0],
        ph.at[1, 0, rest],
        ph.at[0, 0, rest],
        ph.at[1, rest, 0],
        ph.at[0, rest, rest, rows_a],
        ph.at[1, rest, rest, rows_a],
        ph.at[0, rest, rest, rows_b],
        ph.at[1, rest, rest, rows_b],
    ]
    for d in ring:
        rcopy(ph.at[0, 0, 0], ph.at[0, d, 0], ph_s.at[0], ph_r.at[0], plane(d, 0)).start()
        rcopy(ph.at[1, 0, 0], ph.at[1, 0, d], ph_s.at[1], ph_r.at[1], plane(0, d)).start()
    for d in ring:
        rcopy(ph.at[0, 0, 0], ph.at[0, 0, d], ph_s.at[2], ph_r.at[2], plane(0, d)).start()
        rcopy(ph.at[1, 0, 0], ph.at[1, d, 0], ph_s.at[3], ph_r.at[3], plane(d, 0)).start()

    def send_pol(first, dx, dy):
        q = 0 if first else 1 + dx
        src, dst = (s1, r1) if first else (s2, r2)
        rcopy(
            src.at[dx, lax.rem(y + dy, Y)], dst.at[dx * 4 + dy],
            pol_s.at[q], pol_r.at[q], plane(dx, dy),
        ).start()

    pltpu.make_async_copy(s1.at[0, y], r1.at[0], in_sem.at[4]).start()
    for dx, dy in offsets:
        k = dx * 4 + dy
        rcopy(tw.at[0], tw.at[k], tw_s.at[0], tw_r.at[0], plane(dx, dy)).start()

    for dx, dy in SPREAD:
        send_pol(True, dx, dy)

    def forward(q, strip, rows):
        for d in ring:
            if strip == 0:
                c = rcopy(
                    ph.at[0, rest, 0, rows], ph.at[0, rest, d, rows],
                    ph_s.at[q], ph_r.at[q], plane(0, d),
                )
            else:
                c = rcopy(
                    ph.at[1, 0, rest, rows], ph.at[1, d, rest, rows],
                    ph_s.at[q], ph_r.at[q], plane(d, 0),
                )
            c.start()

    wait_for(arrive[0], ph_r.at[0])
    forward(4, 0, rows_a)
    wait_for(arrive[1], ph_r.at[1])
    forward(5, 1, rows_a)
    forward(6, 0, rows_b)
    forward(7, 1, rows_b)

    for dx in near_x:
        relayout(False, dx)
    pltpu.make_async_copy(s2.at[0, y], r2.at[0], in_sem.at[5]).start()

    wait_for(tw.at[pl.ds(1, 15)], tw_r.at[0])
    tots[0] = jnp.sum(tw[...], axis=0)
    ct = rcopy(tots.at[0], tots.at[1], t_s.at[0], t_r.at[0], core_peer)
    ct.start()

    def contract(first, half, xs, cc):
        src = r1 if first else r2
        at = 0 if half == 0 else ROWS1
        def taken(ref, rows):
            return jnp.concatenate(
                [ref[4 * dx : 4 * dx + 4, rows].reshape(-1, 128) for dx in xs], axis=0
            )

        def columns(lo):
            return taken(src, pl.ds(pl.multiple_of(cc * 2 * BODY + lo, 16), BODY))

        w0, w1 = columns(0), columns(BODY)
        count = 4 * len(xs)
        lt = taken(src, slice(4 * BODY, POL_ROWS)).astype(F32).reshape(count, 16, 128)
        lt = jnp.where(cc == 0, lt[:, :8], lt[:, 8:]).reshape(-1, 128).astype(BF16)

        def lanes(lo, hi):
            return jnp.concatenate(
                [
                    jnp.concatenate([ph[s, dx, :, lo:hi].reshape(-1, 128) for dx in xs], axis=0)
                    for s in range(2)
                ],
                axis=1,
            )

        pr = lanes(at, at + BODY)
        pi = lanes(at + BODY, at + 2 * BODY)
        pt = lanes(2 * BODY, ROWS1).reshape(count, 16, 256).astype(F32)
        pt = pt[:, :8] if half == 0 else pt[:, 8:]
        turned = jnp.concatenate([-pt[:, 4:], pt[:, :4]], axis=1)
        pt = pt.reshape(-1, 256).astype(BF16)
        turned = turned.reshape(-1, 256).astype(BF16)
        yield tdot(w0, pr) - tdot(w1, pi) + tdot(lt, pt)
        yield tdot(w0, pi) + tdot(w1, pr) + tdot(lt, turned)

    mine = pl.multiple_of(core * 128, 128)
    theirs = pl.multiple_of((1 - core) * 128, 128)

    def sums(first, half, xs, cc, add):
        rows = pl.ds(pl.multiple_of(cc * 128, 128), 128)
        for k, value in enumerate(contract(first, half, xs, cc)):
            n = (0 if first else 4) + half * 2 + k
            part[n, rows] = part[n, rows] + value if add else value
            yield n

    def spread(first, half):
        xs = range(X) if first else (0, 2)
        copies = []
        for n in sums(first, half, xs, 1 - core, not first):
            c = rcopy(part.at[n, pl.ds(theirs, 128)], d2d.at[n], d_s.at[n], d_r.at[n], core_peer)
            c.start()
            copies.append(c)
        for _ in sums(first, half, xs, core, not first):
            pass
        return copies

    d_copies, z_copies = [], []
    for g in (2, 3, 4, 5):
        wait_for(arrive[g], ph_r.at[g])
    for dx, dy in SPREAD:
        send_pol(False, dx, dy)
    wait_for(r1.at[pl.ds(1, 15)], pol_r.at[0])
    wait_for(r1.at[0], in_sem.at[4])
    @pl.when(zh == 0)
    def _():
        pl.semaphore_wait(ready, 1)

    for half in range(2):
        if half == 1:
            for g in (6, 7):
                wait_for(arrive[g], ph_r.at[g])
        d_copies += spread(True, half)
        if half == 0:
            ct.wait_recv()
            tots[2] = tots[0] + tots[1]
            cz = rcopy(tots.at[2], tots.at[3], t_s.at[1], t_r.at[1], z_peer)
            cz.start()
        for n in (half * 2, half * 2 + 1):
            d_copies[n].wait_recv()
            zsend[n] = (part[n, pl.ds(mine, 128)] + d2d[n]).astype(BF16)
            c = rcopy(zsend.at[n], zrecv.at[n], z_s.at[n], z_r.at[n], z_peer)
            c.start()
            z_copies.append(c)

    own_slots = [pl.ds(1, 3)] + [pl.ds(4 * dx, 4) for dx in range(1, X)]
    for dx in (1, 3):
        wait_for(r2.at[own_slots[dx]], pol_r.at[1 + dx])
    for half in range(2):
        for cc in (1 - core, core):
            for _ in sums(False, half, (1, 3), cc, False):
                pass
    for dx in (0, 2):
        wait_for(r2.at[own_slots[dx]], pol_r.at[1 + dx])
    wait_for(r2.at[0], in_sem.at[5])
    d_copies += spread(False, 0) + spread(False, 1)
    cz.wait_recv()
    total = tots[2] + tots[3]
    ri = lax.broadcasted_iota(jnp.int32, (128, 128), 0)
    ci = lax.broadcasted_iota(jnp.int32, (128, 128), 1)
    column = jnp.sum(jnp.where(ri == ci, total, 0.0), axis=1, keepdims=True)
    for half in range(2):
        rows = 0.0
        for k in range(2):
            n = half * 2 + k
            z_copies[n].wait_recv()
            d_copies[4 + n].wait_recv()
            summed = part[4 + n, pl.ds(mine, 128)] + d2d[4 + n] + zrecv[n].astype(F32)
            value = (summed / column).astype(BF16)
            rows = rows + jnp.dot(order_o[k], value, preferred_element_type=F32)
        out[:, :, pl.ds(half * 256, 256)] = rows.astype(BF16).reshape(128, 2, 256)

    for c in [ct, cz] + d_copies + z_copies:
        c.wait_send()
    for g in range(8):
        wait_for(arrive[g], ph_s.at[g])
    wait_for(r1.at[pl.ds(1, 15)], pol_s.at[0])
    for dx in range(X):
        wait_for(r2.at[own_slots[dx]], pol_s.at[1 + dx])
    wait_for(tw.at[pl.ds(1, 15)], tw_s.at[0])


def body(pol_cube, phasor, chan_weight, flags):
    vmem = pltpu.VMEM
    dma = pltpu.SemaphoreType.DMA
    out = pl.pallas_call(
        kernel,
        out_shape=jax.ShapeDtypeStruct((128, 2, 512), BF16),
        in_specs=[pl.BlockSpec(memory_space=pltpu.HBM)] * 4,
        out_specs=pl.BlockSpec(memory_space=vmem),
        scratch_shapes=[
            vmem((2, CH, 8, 1024), BF16),
            vmem((CH, 2, 512), BF16),
            vmem((1, CH), F32),
            vmem((8, CH), jnp.int32),
            vmem((2, 256, 128), BF16),
            vmem((CH, 8, 128), F32),
            vmem((X, Y, POL_ROWS, 128), BF16),
            vmem((X, Y, POL_ROWS, 128), BF16),
            vmem((16, POL_ROWS, 128), BF16),
            vmem((16, POL_ROWS, 128), BF16),
            vmem((2, X, Y, PH_ROWS, 128), BF16),
            vmem((16, 1, 128), F32),
            vmem((8, 256, 256), F32),
            vmem((8, 128, 256), F32),
            vmem((4, 128, 256), BF16),
            vmem((4, 128, 256), BF16),
            vmem((4, 1, 128), F32),
            dma((6,)),
            dma((5,)), dma((5,)),
            dma((8,)), dma((8,)),
            dma((1,)), dma((1,)),
            dma((8,)), dma((8,)),
            dma((4,)), dma((4,)),
            dma((2,)), dma((2,)),
            pltpu.SemaphoreType.REGULAR,
        ],
        compiler_params=pltpu.CompilerParams(
            collective_id=0, has_side_effects=True, vmem_limit_bytes=40 * 2**20
        ),
        cost_estimate=pl.CostEstimate(
            flops=2 * 512 * 1152 * 1024, bytes_accessed=2**21, transcendentals=0
        ),
        name="exchange",
    )(*[pltpu.with_memory_space_constraint(a, pltpu.HBM) for a in (pol_cube, phasor.transpose(1, 0, 2), chan_weight[None, :], flags.T)])
    return out.reshape(1, 16, 8, 2, 512)


def solution(mesh):
    placed = (P(None, "chan", None, "pix"), P(None, "chan", None), P("chan"), P("chan", None))
    return jax.shard_map(
        body,
        mesh=mesh,
        in_specs=placed,
        out_specs=P("pix", "chan", None, None, None),
        check_vma=False,
    )
```

```python
import jax
import jax.numpy as jnp
from jax import lax
from jax.experimental import pallas as pl
from jax.experimental.pallas import tpu as pltpu
from jax.sharding import PartitionSpec as P

MESH = pl.DeviceIdType.MESH
F32 = jnp.float32
BF16 = jnp.bfloat16

X, Y = 4, 4
SPREAD = [(dx, dy) for dx in (1, 3, 0, 2) for dy in range(Y) if dx or dy]
FAR = sorted(SPREAD, key=lambda o: -(0, 1, 2, 1)[o[0]] - (0, 1, 2, 1)[o[1]])
CH = 36
BODY = 32
ROWS1 = 2 * BODY + 16
ROWS2 = 2 * BODY
PH_ROWS = ROWS1 + ROWS2
POL_ROWS = 4 * BODY + 16


def tdot(a, b):
    return lax.dot_general(a, b, (((0,), (0,)), ((), ())), preferred_element_type=F32)


def kernel(
    pol_hbm, phasor_hbm, cw_hbm, flags_hbm, out,
    pol, phasor, cw, flags_t, order_o, wb, s1, s2, r1, r2, ph, tw, part, d2d, zsend, zrecv, tots,
    in_sem, pol_s, pol_r, ph_s, ph_r, tw_s, tw_r, d_s, d_r, z_s, z_r, t_s, t_r, ready,
):
    me = lax.axis_index("chan")
    pix = lax.axis_index("pix")
    core = lax.rem(me, 2)
    y = lax.rem(me // 2, Y)
    x = lax.rem(me // (2 * Y), X)
    zh = me // (2 * X * Y)

    def dev(zz, xx, yy, cc):
        return (((zz * X + xx) * Y + yy) * 2 + cc, pix)

    def plane(dx, dy):
        return dev(zh, lax.rem(x + dx, X), lax.rem(y + dy, Y), core)

    core_peer = dev(zh, x, y, 1 - core)
    z_peer = dev(1 - zh, x, y, core)
    offsets = [(dx, dy) for dx in range(X) for dy in range(Y) if dx or dy]

    barrier = pltpu.get_barrier_semaphore()
    peers = [plane(dx, dy) for dx, dy in offsets] + [core_peer]
    for target in peers:
        pl.semaphore_signal(barrier, inc=1, device_id=target, device_id_type=MESH)

    @pl.when(zh == 0)
    def _():
        pl.semaphore_signal(barrier, inc=1, device_id=z_peer, device_id_type=MESH)

    loads = [
        pltpu.make_async_copy(a, b, in_sem.at[i])
        for i, (a, b) in enumerate(
            ((flags_hbm, flags_t), (cw_hbm, cw), (phasor_hbm, phasor), (pol_hbm, pol))
        )
    ]
    for c in loads:
        c.start()

    i = lax.broadcasted_iota(jnp.int32, (256, 256), 0)
    j = lax.broadcasted_iota(jnp.int32, (256, 256), 1)
    order = jnp.where((i % 32) * 8 + i // 32 == j, 1.0, 0.0).astype(BF16)
    i, j = i[:64, :64], j[:64, :64]
    order_t = jnp.where((i % 8) * 8 + i // 8 == j, 1.0, 0.0).astype(BF16)

    i = lax.broadcasted_iota(jnp.int32, (256, 128), 0)
    j = lax.broadcasted_iota(jnp.int32, (256, 128), 1)
    at_row = (i // 2) % 8 * 16 + i // 16 == j
    for k in range(2):
        order_o[k] = jnp.where(at_row & (i % 2 == k), 1.0, 0.0).astype(BF16)

    loads[0].wait()
    loads[1].wait()
    w = cw[...] * flags_t[...].astype(F32)
    for c in range(CH):
        wb[c] = jnp.broadcast_to(w[:, c : c + 1], (8, 128))
    row_sum = jnp.sum(w, axis=1, keepdims=True)
    lane = lax.broadcasted_iota(jnp.int32, (8, 128), 1)
    sub = lax.broadcasted_iota(jnp.int32, (8, 128), 0)
    tw[0] = jnp.sum(jnp.where(lane // 16 == sub, row_sum, 0.0), axis=0, keepdims=True)

    loads[2].wait()
    both = phasor[...].astype(F32)
    re, im = both[:, 0], both[:, 1]
    tails = [jnp.concatenate([re[BODY:, h : h + 256], -im[BODY:, h : h + 256]], axis=0) for h in (0, 256)]
    block = jnp.concatenate(
        [re[:BODY, :256], im[:BODY, :256]] + tails + [re[:BODY, 256:], im[:BODY, 256:]], axis=0
    ).astype(BF16)
    ph[0, 0, 0] = block[:, :128]
    ph[1, 0, 0] = block[:, 128:]

    lane_b = lax.broadcasted_iota(jnp.int32, (1, 128), 1)

    def swap_blocks(v):
        for k in range(3):
            m = 1 << k
            mask = jnp.broadcast_to((lane_b // (16 * m)) % 2 == 1, v[0].shape)
            new = list(v)
            for a in range(8):
                if a & m:
                    continue
                b = a | m
                new[a] = jnp.where(mask, pltpu.roll(v[b], 16 * m, 1), v[a])
                new[b] = jnp.where(mask, v[b], pltpu.roll(v[a], 128 - 16 * m, 1))
            v = new
        return v

    def weighted(s, chans, at):
        v = pol[s, chans, :, pl.ds(at, 128)].astype(F32) * wb[chans]
        return v.reshape(-1, 128).astype(BF16)

    def regroup(matrix, v, rows, kind):
        u = jnp.dot(matrix, v, preferred_element_type=F32).astype(kind)
        return swap_blocks([u[r * rows : (r + 1) * rows] for r in range(8)])

    def relayout(first, dx):
        xx = lax.rem(x + dx, X)
        at = pl.multiple_of(((1 - zh if first else zh) * X + xx) * 128, 128)
        dst = s1 if first else s2
        for s in range(2):
            v = regroup(order, weighted(s, slice(0, BODY), at), BODY, BF16)
            for g in range(8):
                dst[dx, g // 2, pl.ds((g % 2) * 2 * BODY + s * BODY, BODY), :] = v[g]
        v = [weighted(s, slice(BODY, CH), at) for s in range(2)]
        v = regroup(order_t, jnp.concatenate(v, axis=0), 8, F32)
        for yy in range(Y):
            tail = jnp.concatenate([v[2 * yy], v[2 * yy + 1]], axis=0)
            dst[dx, yy, pl.ds(4 * BODY, 16), :] = tail.astype(BF16)

    loads[3].wait()
    near_x = (1, 3, 0, 2)
    for dx in near_x:
        relayout(True, dx)

    pl.semaphore_wait(barrier, len(peers) + zh)

    @pl.when(zh == 1)
    def _():
        pl.semaphore_signal(ready, inc=1, device_id=z_peer, device_id_type=MESH)

    def rcopy(src, dst, ss, rs, target):
        return pltpu.make_async_remote_copy(
            src_ref=src, dst_ref=dst, send_sem=ss, recv_sem=rs,
            device_id=target, device_id_type=MESH,
        )

    def wait_for(view, sem):
        pltpu.make_async_copy(view, view, sem).wait()

    ring = (2, 1, 3)
    rest = pl.ds(1, 3)
    rows_a, rows_b = pl.ds(0, ROWS1), pl.ds(ROWS1, ROWS2)
    arrive = [
        ph.at[0, rest, 0],
        ph.at[1, 0, rest],
        ph.at[0, 0, rest],
        ph.at[1, rest, 0],
        ph.at[0, rest, rest, rows_a],
        ph.at[1, rest, rest, rows_a],
        ph.at[0, rest, rest, rows_b],
        ph.at[1, rest, rest, rows_b],
    ]
    for d in ring:
        rcopy(ph.at[0, 0, 0], ph.at[0, d, 0], ph_s.at[0], ph_r.at[0], plane(d, 0)).start()
        rcopy(ph.at[1, 0, 0], ph.at[1, 0, d], ph_s.at[1], ph_r.at[1], plane(0, d)).start()
    for d in ring:
        rcopy(ph.at[0, 0, 0], ph.at[0, 0, d], ph_s.at[2], ph_r.at[2], plane(0, d)).start()
        rcopy(ph.at[1, 0, 0], ph.at[1, d, 0], ph_s.at[3], ph_r.at[3], plane(d, 0)).start()

    def send_pol(first, dx, dy):
        q = 0 if first else 1 + dx
        src, dst = (s1, r1) if first else (s2, r2)
        rcopy(
            src.at[dx, lax.rem(y + dy, Y)], dst.at[dx * 4 + dy],
            pol_s.at[q], pol_r.at[q], plane(dx, dy),
        ).start()

    pltpu.make_async_copy(s1.at[0, y], r1.at[0], in_sem.at[4]).start()
    for dx, dy in offsets:
        k = dx * 4 + dy
        rcopy(tw.at[0], tw.at[k], tw_s.at[0], tw_r.at[0], plane(dx, dy)).start()

    for dx, dy in FAR:
        send_pol(True, dx, dy)

    def forward(q, strip, rows):
        for d in ring:
            if strip == 0:
                c = rcopy(
                    ph.at[0, rest, 0, rows], ph.at[0, rest, d, rows],
                    ph_s.at[q], ph_r.at[q], plane(0, d),
                )
            else:
                c = rcopy(
                    ph.at[1, 0, rest, rows], ph.at[1, d, rest, rows],
                    ph_s.at[q], ph_r.at[q], plane(d, 0),
                )
            c.start()

    wait_for(arrive[0], ph_r.at[0])
    forward(4, 0, rows_a)
    wait_for(arrive[1], ph_r.at[1])
    forward(5, 1, rows_a)
    forward(6, 0, rows_b)
    forward(7, 1, rows_b)

    for dx in near_x:
        relayout(False, dx)
    pltpu.make_async_copy(s2.at[0, y], r2.at[0], in_sem.at[5]).start()

    wait_for(tw.at[pl.ds(1, 15)], tw_r.at[0])
    tots[0] = jnp.sum(tw[...], axis=0)
    ct = rcopy(tots.at[0], tots.at[1], t_s.at[0], t_r.at[0], core_peer)
    ct.start()

    def contract(first, half, xs, cc):
        src = r1 if first else r2
        at = 0 if half == 0 else ROWS1
        def taken(ref, rows):
            return jnp.concatenate(
                [ref[4 * dx : 4 * dx + 4, rows].reshape(-1, 128) for dx in xs], axis=0
            )

        def columns(lo):
            return taken(src, pl.ds(pl.multiple_of(cc * 2 * BODY + lo, 16), BODY))

        w0, w1 = columns(0), columns(BODY)
        count = 4 * len(xs)
        lt = taken(src, slice(4 * BODY, POL_ROWS)).astype(F32).reshape(count, 16, 128)
        lt = jnp.where(cc == 0, lt[:, :8], lt[:, 8:]).reshape(-1, 128).astype(BF16)

        def lanes(lo, hi):
            return jnp.concatenate(
                [
                    jnp.concatenate([ph[s, dx, :, lo:hi].reshape(-1, 128) for dx in xs], axis=0)
                    for s in range(2)
                ],
                axis=1,
            )

        pr = lanes(at, at + BODY)
        pi = lanes(at + BODY, at + 2 * BODY)
        pt = lanes(2 * BODY, ROWS1).reshape(count, 16, 256).astype(F32)
        pt = pt[:, :8] if half == 0 else pt[:, 8:]
        turned = jnp.concatenate([-pt[:, 4:], pt[:, :4]], axis=1)
        pt = pt.reshape(-1, 256).astype(BF16)
        turned = turned.reshape(-1, 256).astype(BF16)
        yield tdot(w0, pr) - tdot(w1, pi) + tdot(lt, pt)
        yield tdot(w0, pi) + tdot(w1, pr) + tdot(lt, turned)

    mine = pl.multiple_of(core * 128, 128)
    theirs = pl.multiple_of((1 - core) * 128, 128)

    def sums(first, half, xs, cc, add):
        rows = pl.ds(pl.multiple_of(cc * 128, 128), 128)
        for k, value in enumerate(contract(first, half, xs, cc)):
            n = (0 if first else 4) + half * 2 + k
            part[n, rows] = part[n, rows] + value if add else value
            yield n

    def spread(first, half):
        xs = range(X) if first else (0, 2)
        copies = []
        for n in sums(first, half, xs, 1 - core, not first):
            c = rcopy(part.at[n, pl.ds(theirs, 128)], d2d.at[n], d_s.at[n], d_r.at[n], core_peer)
            c.start()
            copies.append(c)
        for _ in sums(first, half, xs, core, not first):
            pass
        return copies

    d_copies, z_copies = [], []
    for g in (2, 3, 4, 5):
        wait_for(arrive[g], ph_r.at[g])
    for dx, dy in SPREAD:
        send_pol(False, dx, dy)
    wait_for(r1.at[pl.ds(1, 15)], pol_r.at[0])
    wait_for(r1.at[0], in_sem.at[4])
    @pl.when(zh == 0)
    def _():
        pl.semaphore_wait(ready, 1)

    for half in range(2):
        if half == 1:
            for g in (6, 7):
                wait_for(arrive[g], ph_r.at[g])
        d_copies += spread(True, half)
        if half == 0:
            ct.wait_recv()
            tots[2] = tots[0] + tots[1]
            cz = rcopy(tots.at[2], tots.at[3], t_s.at[1], t_r.at[1], z_peer)
            cz.start()
        for n in (half * 2, half * 2 + 1):
            d_copies[n].wait_recv()
            zsend[n] = (part[n, pl.ds(mine, 128)] + d2d[n]).astype(BF16)
            c = rcopy(zsend.at[n], zrecv.at[n], z_s.at[n], z_r.at[n], z_peer)
            c.start()
            z_copies.append(c)

    own_slots = [pl.ds(1, 3)] + [pl.ds(4 * dx, 4) for dx in range(1, X)]
    for dx in (1, 3):
        wait_for(r2.at[own_slots[dx]], pol_r.at[1 + dx])
    for half in range(2):
        for cc in (1 - core, core):
            for _ in sums(False, half, (1, 3), cc, False):
                pass
    for dx in (0, 2):
        wait_for(r2.at[own_slots[dx]], pol_r.at[1 + dx])
    wait_for(r2.at[0], in_sem.at[5])
    d_copies += spread(False, 0) + spread(False, 1)
    cz.wait_recv()
    total = tots[2] + tots[3]
    ri = lax.broadcasted_iota(jnp.int32, (128, 128), 0)
    ci = lax.broadcasted_iota(jnp.int32, (128, 128), 1)
    column = jnp.sum(jnp.where(ri == ci, total, 0.0), axis=1, keepdims=True)
    for half in range(2):
        rows = 0.0
        for k in range(2):
            n = half * 2 + k
            z_copies[n].wait_recv()
            d_copies[4 + n].wait_recv()
            summed = part[4 + n, pl.ds(mine, 128)] + d2d[4 + n] + zrecv[n].astype(F32)
            value = (summed / column).astype(BF16)
            rows = rows + jnp.dot(order_o[k], value, preferred_element_type=F32)
        out[:, :, pl.ds(half * 256, 256)] = rows.astype(BF16).reshape(128, 2, 256)

    for c in [ct, cz] + d_copies + z_copies:
        c.wait_send()
    for g in range(8):
        wait_for(arrive[g], ph_s.at[g])
    wait_for(r1.at[pl.ds(1, 15)], pol_s.at[0])
    for dx in range(X):
        wait_for(r2.at[own_slots[dx]], pol_s.at[1 + dx])
    wait_for(tw.at[pl.ds(1, 15)], tw_s.at[0])


def body(pol_cube, phasor, chan_weight, flags):
    vmem = pltpu.VMEM
    dma = pltpu.SemaphoreType.DMA
    out = pl.pallas_call(
        kernel,
        out_shape=jax.ShapeDtypeStruct((128, 2, 512), BF16),
        in_specs=[pl.BlockSpec(memory_space=pltpu.HBM)] * 4,
        out_specs=pl.BlockSpec(memory_space=vmem),
        scratch_shapes=[
            vmem((2, CH, 8, 1024), BF16),
            vmem((CH, 2, 512), BF16),
            vmem((1, CH), F32),
            vmem((8, CH), jnp.int32),
            vmem((2, 256, 128), BF16),
            vmem((CH, 8, 128), F32),
            vmem((X, Y, POL_ROWS, 128), BF16),
            vmem((X, Y, POL_ROWS, 128), BF16),
            vmem((16, POL_ROWS, 128), BF16),
            vmem((16, POL_ROWS, 128), BF16),
            vmem((2, X, Y, PH_ROWS, 128), BF16),
            vmem((16, 1, 128), F32),
            vmem((8, 256, 256), F32),
            vmem((8, 128, 256), F32),
            vmem((4, 128, 256), BF16),
            vmem((4, 128, 256), BF16),
            vmem((4, 1, 128), F32),
            dma((6,)),
            dma((5,)), dma((5,)),
            dma((8,)), dma((8,)),
            dma((1,)), dma((1,)),
            dma((8,)), dma((8,)),
            dma((4,)), dma((4,)),
            dma((2,)), dma((2,)),
            pltpu.SemaphoreType.REGULAR,
        ],
        compiler_params=pltpu.CompilerParams(
            collective_id=0, has_side_effects=True, vmem_limit_bytes=40 * 2**20
        ),
        cost_estimate=pl.CostEstimate(
            flops=2 * 512 * 1152 * 1024, bytes_accessed=2**21, transcendentals=0
        ),
        name="exchange",
    )(*[pltpu.with_memory_space_constraint(a, pltpu.HBM) for a in (pol_cube, phasor.transpose(1, 0, 2), chan_weight[None, :], flags.T)])
    return out.reshape(1, 16, 8, 2, 512)


def solution(mesh):
    placed = (P(None, "chan", None, "pix"), P(None, "chan", None), P("chan"), P("chan", None))
    return jax.shard_map(
        body,
        mesh=mesh,
        in_specs=placed,
        out_specs=P("pix", "chan", None, None, None),
        check_vma=False,
    )
```
